256 devices in a mesh: comp: 8 (over z_hi, y), brick: 32 (over x, z_lo, core).
Axes of the slice: x: 4, y: 4, z: 8 (z_hi: 2, z_lo: 4; z = z_hi * 4 + z_lo), core: 2. Of those that a mesh axis runs over, the one named last changes fastest.
Arguments:
- initial: float32 [8, 16, 16, 16, 4096], P('comp', None, None, None, 'brick'), may hold values from -6 to 6
- levels: int32 [8, 4], P('comp'), may hold values from 1 to 6
- weights: int32 [8], P('comp'), may hold values from -1 to 1, as said below
- velocity: float32 [4], replicated, may hold values from 0.2 to 2
- diffusivity: float32 [4], replicated, may hold values from 0.01 to 0.1
Outputs:
- combined: float32 [16, 16, 16, 4096], P(None, None, None, 'brick')
The draws below stay inside these ranges and needn't reach their ends.
Inputs may be any that keep to these rules, and one draw needn't show every extreme that they name: `weights`: each coefficient is -1 or +1, both signs occur.
All inputs are finite; a program needn't handle non-finite values.
Results may differ from the reference program's by a relative error of at most 0.0001.
Values sent between devices are 32-bit elements; how exact they have to be, the bound alone decides.
No kernel may reach another device: no remote copies, remote signals or barrier semaphores. Data moves between devices by JAX's collectives and lax.ppermute only.
A program may use at most 192 MiB of HBM per device.

```python
import math
import jax
import jax.numpy as jnp

N1 = 16
N2 = 16
N3 = 16
NZ = 4096
COMPS = 8


def draw_weights(key, part):
    key = jax.random.fold_in(key, 5)
    order = jax.random.permutation(key, COMPS)
    return jnp.where(order < (COMPS + 1) // 2, 1, -1).astype(jnp.int32)


def place_ends(values, stream_key, smallest, largest):
    place = [jax.random.randint(jax.random.fold_in(stream_key, axis), (), 0, length) for axis, length in enumerate(values.shape)]
    widest = values.shape.index(max(values.shape))
    neighbour = place[:widest] + [(place[widest] + 1) % values.shape[widest]] + place[widest + 1:]
    return values.at[tuple(place)].set(smallest).at[tuple(neighbour)].set(largest)


def steps_of(rng, dims, split, smallest, top_value):
    def one(axis_at, blocks):
        draws = jax.random.uniform(jax.random.fold_in(jax.random.fold_in(rng, 6), axis_at), (blocks,), jnp.float32, smallest / len(split), top_value / len(split))
        return jnp.repeat(jnp.exp(draws), dims[axis_at] // blocks).reshape((-1,) + (1,) * (len(dims) - axis_at - 1))

    factor_of = one(*split[0])
    for cut in split[1:]:
        factor_of = factor_of * one(*cut)
    return factor_of


def normal_values(own_key, shape, spread, most, cuts=(), kind=jnp.bfloat16):
    loudness = steps_of(own_key, shape, cuts, -0.22, 0.18) if cuts else 1.0
    entries = jax.random.normal(own_key, shape, jnp.float32) * spread * loudness
    return jnp.minimum(jnp.maximum(entries, -most), most).astype(kind)


def setup_inputs(seed: int = 0) -> dict:
    key_list = jax.random.split(jax.random.key(seed), 6)
    initial = normal_values(key_list[0], (COMPS, N1, N2, N3, NZ), 1.0, 6.0, ((0, 8), (4, 32)), jnp.float32)
    levels = place_ends(jax.random.randint(key_list[1], (COMPS, 4), 1, 7), jax.random.fold_in(key_list[1], 1), 1, 6).astype(jnp.int32)
    weights = draw_weights(jax.random.fold_in(key_list[5], 71), 0)
    velocity = jnp.clip(jnp.exp(jax.random.uniform(key_list[3], (4,), jnp.float32, math.log(0.2), math.log(2.0))), 0.2, 2.0)
    diffusivity = jnp.clip(jnp.exp(jax.random.uniform(key_list[4], (4,), jnp.float32, math.log(0.01), math.log(0.1))), 0.01, 0.1)
    return dict(initial=initial, levels=levels, weights=weights, velocity=velocity, diffusivity=diffusivity)


cfl_limit = 0.9


def step_factors(level, velocity, diffusivity):
    inverse = jnp.exp2(level.astype(jnp.float32))
    total = jnp.sum(velocity * inverse + 2.0 * diffusivity * inverse * inverse)
    delta = cfl_limit / total
    return delta * velocity * inverse, delta * diffusivity * inverse * inverse


def substep(field, advect, diffuse):
    result = field
    for axis_num in range(4):
        lower = jnp.roll(field, 1, axis=axis_num)
        upper = jnp.roll(field, -1, axis=axis_num)
        result = result - advect[axis_num] * (field - lower) + diffuse[axis_num] * (upper - 2.0 * field + lower)
    return result


def hierarchize(field):
    count = field.shape[-1]
    index = jnp.arange(count, dtype=jnp.int32)
    lowbit = jnp.bitwise_and(index, -index)
    below = jnp.take(field, jnp.mod(index - lowbit, count).astype(jnp.int32), axis=-1)
    above = jnp.take(field, jnp.mod(index + lowbit, count).astype(jnp.int32), axis=-1)
    return jnp.where(index == 0, field, field - 0.5 * (below + above))


def reference(initial, levels, weights, velocity, diffusivity):
    total = jnp.zeros(initial.shape[1:], jnp.float32)
    for group in range(COMPS):
        advect, diffuse = step_factors(levels[group], velocity, diffusivity)
        field = initial[group]
        field = substep(field, advect, diffuse)
        field = substep(field, advect, diffuse)
        total = total + weights[group].astype(jnp.float32) * hierarchize(field)
    return total
```

```python
import functools
import jax
import jax.numpy as jnp
import numpy as np
from jax import lax
from jax.experimental import pallas as pl
from jax.experimental.pallas import tpu as pltpu
from jax.sharding import Mesh, PartitionSpec as P

cfl_limit = 0.9
BRICK = ("x", "zl", "core")
HI = lax.Precision.HIGHEST
VM = pl.BlockSpec(memory_space=pltpu.VMEM)
SM = pl.BlockSpec(memory_space=pltpu.SMEM)
F32 = jnp.float32


def compiler_params():
    return pltpu.CompilerParams(vmem_limit_bytes=40 * 1024 * 1024)


def factors(lev, vel, dif):
    inv = [jnp.left_shift(1, lev[0, d]).astype(F32) for d in range(4)]
    total = sum(vel[d] * inv[d] + 2.0 * dif[d] * inv[d] * inv[d] for d in range(4))
    delta = cfl_limit / jnp.full((1, 128), total, F32)
    adv = [delta * (vel[d] * inv[d]) for d in range(4)]
    dfs = [delta * (dif[d] * inv[d] * inv[d]) for d in range(4)]
    center = 1.0 - sum(adv[d] + 2.0 * dfs[d] for d in range(4))
    return center, [adv[d] + dfs[d] for d in range(4)], dfs


def lane_id(shape):
    return lax.broadcasted_iota(jnp.int32, shape, len(shape) - 1)


def lane_factors(lo, hi):
    lane = lane_id((1, 128))
    return jnp.where(lane == 0, 0.0, lo), jnp.where(lane == 127, 0.0, hi)


def step_row(ref, p, i, fac):
    center, lo, hi, lo3, hi3 = fac
    before, after = lax.rem(p + 15, 16), lax.rem(p + 1, 16)
    u = ref[p, i]
    out = center * u + lo[0] * ref[before, i] + hi[0] * ref[after, i]
    out = out + lo[1] * ref[p, (i + 15) % 16] + hi[1] * ref[p, (i + 1) % 16]
    out = out + lo[2] * pltpu.roll(u, 1, 0) + hi[2] * pltpu.roll(u, 15, 0)
    return out + lo3 * pltpu.roll(u, 1, 1) + hi3 * pltpu.roll(u, 127, 1)


def ends_kernel(x_ref, lo_ref, hi_ref):
    row = lax.broadcasted_iota(jnp.int32, (8, 128), 0)
    lane = lane_id((8, 128))
    want = jnp.where(row < 2, row, row + 124)
    pick = jnp.where((lane == want) & (row < 4), 1.0, 0.0).astype(F32)
    for c in range(32):
        block = x_ref[c // 2, 8 * (c % 2) : 8 * (c % 2) + 8].reshape(128, 128)
        got = lax.dot_general(pick, block, (((1,), (1,)), ((), ())), precision=HI, preferred_element_type=F32)
        at = (slice(c // 2, c // 2 + 1), slice(128 * (c % 2), 128 * (c % 2) + 128))
        lo_ref[0, at[0], at[1]] = got[0:1]
        lo_ref[1, at[0], at[1]] = got[1:2]
        hi_ref[0, at[0], at[1]] = got[2:3]
        hi_ref[1, at[0], at[1]] = got[3:4]


def first_kernel(lev, vel, dif, x_ref, u_ref):
    center, lo, hi = factors(lev, vel, dif)
    fac = (center, lo, hi) + lane_factors(lo[3], hi[3])

    def plane(p, _):
        for i in range(16):
            u_ref[p, i] = step_row(x_ref, p, i, fac)
        return 0

    lax.fori_loop(0, 16, plane, 0)


def layer_step(u, below, above, center, lo, hi):
    def wide(v):
        return jnp.concatenate([v, v], axis=1)

    lane = lane_id((16, 256)) & 15
    out = wide(center) * u + wide(lo[0]) * pltpu.roll(u, 1, 0) + wide(hi[0]) * pltpu.roll(u, 15, 0)
    out = out + wide(lo[1]) * pltpu.roll(u, 16, 1) + wide(hi[1]) * pltpu.roll(u, 240, 1)
    down = jnp.where(lane == 0, pltpu.roll(u, 241, 1), pltpu.roll(u, 1, 1))
    up = jnp.where(lane == 15, pltpu.roll(u, 15, 1), pltpu.roll(u, 255, 1))
    out = out + wide(lo[2]) * down + wide(hi[2]) * up
    return out + wide(lo[3]) * below + wide(hi[3]) * above


def spread(pair, ends):
    return lax.dot_general(pair, ends, (((0,), (0,)), ((), ())), precision=HI, preferred_element_type=F32)


def quarters(y):
    a1 = jnp.where((y == 1) | (y == 2), 1, 0)
    return a1, lax.shift_right_logical(y, 1)


def second_kernel(lev, vel, dif, wgt, pos, u_ref, lo_ref, hi_ref, left_ref, right_ref, *rest):
    outs, (first_ref, full_ref, halo_ref) = rest[:8], rest[8:]
    center, lo, hi = factors(lev, vel, dif)
    fac = (center, lo, hi) + lane_factors(lo[3], hi[3])
    below = layer_step(left_ref[1], left_ref[0], lo_ref[0], center, lo, hi)
    above = layer_step(right_ref[0], hi_ref[1], right_ref[1], center, lo, hi)
    halo_ref[...] = jnp.zeros_like(halo_ref)
    lows, highs = (left_ref[1], below), (right_ref[0], above)
    for s in range(2):
        for c in range(32):
            at = (slice(c // 2, c // 2 + 1), slice(128 * (c % 2), 128 * (c % 2) + 128))
            halo_ref[s, c, 0:1, :] = lows[s][at]
            halo_ref[s, c, 1:2, :] = highs[s][at]
    row = lax.broadcasted_iota(jnp.int32, (8, 128), 0)
    lane = lane_id((8, 128))
    ends = jnp.where((row == 0) & (lane == 0), lo[3], 0.0) + jnp.where((row == 1) & (lane == 127), hi[3], 0.0)

    def mend(c, _):
        p, h = lax.div(c, 2), lax.rem(c, 2)
        at = pl.ds(h * 8, 8)
        full_ref[p, at] = u_ref[p, at] + spread(halo_ref[0, c], ends).reshape(8, 16, 128)
        return 0

    lax.fori_loop(0, 32, mend, 0)
    weight = wgt[0].astype(F32)
    pick = jnp.where((row == 0) & (lane == 0), 1.0, 0.0).astype(F32)
    a1, a2 = quarters(pos[0])

    def plane(p, out_ref, slot):
        got = []
        for h in range(2):
            edge = spread(halo_ref[1, 2 * p + h], ends)
            rows = []
            for i in range(8):
                v = weight * (step_row(full_ref, p, 8 * h + i, fac) + edge[16 * i : 16 * i + 16])
                out_ref[slot, 128 * h + 16 * i : 128 * h + 16 * i + 16, :] = v
                rows.append(v)
            block = jnp.concatenate(rows, axis=0)
            got.append(lax.dot_general(pick, block, (((1,), (1,)), ((), ())), precision=HI, preferred_element_type=F32)[0:1])
        first_ref[pl.ds(p, 1), :] = jnp.concatenate(got, axis=1)

    for n, out_ref in enumerate(outs):
        chunk, which, keep = n // 4, (n // 2) % 2, n % 2
        big, small = (a2, a1) if which else (a1, a2)

        def body(r, _, out_ref=out_ref, chunk=chunk, which=which, keep=keep, big=big, small=small):
            half = big if keep else 1 - big
            bit = jnp.where(r == 1, small, 1 - small)
            plane(8 * chunk + 4 * which + 2 * half + bit, out_ref, r)
            return 0

        lax.fori_loop(0, 2, body, 0)


def surplus_kernel(a_ref, b_ref, mat_ref, o_ref):
    for n in range(a_ref.shape[0]):
        o_ref[n] = jnp.dot(a_ref[n] + b_ref[n], mat_ref[...], precision=HI, preferred_element_type=F32)


def last_kernel(rounds, pos, table, *refs):
    got, rest = refs[:rounds], refs[rounds:]
    pieces, (out_ref, fix_ref) = rest[:-2], rest[-2:]
    b = pos[1]
    near = sum(table[0, b, r] * got[r][...] for r in range(rounds))
    first = sum(table[1, b, r] * got[r][...] for r in range(rounds))
    fix_ref[...] = jnp.zeros_like(fix_ref)
    for c in range(32):
        at = (slice(c // 2, c // 2 + 1), slice(128 * (c % 2), 128 * (c % 2) + 128))
        fix_ref[c, 0:1, :] = near[at]
        fix_ref[c, 1:2, :] = first[at]
    row = lax.broadcasted_iota(jnp.int32, (8, 128), 0)
    lane = lane_id((8, 128))
    gap = 128 - lane
    tail = (lane > 0) & ((gap & (gap - 1)) == 0)
    ends = jnp.where((row == 0) & tail, -0.5, 0.0) + jnp.where((row == 1) & (lane == 0), 1.0, 0.0)
    a1, a2 = quarters(pos[0])
    for chunk in range(2):
        own, one, three, far_a, far_b = pieces[5 * chunk : 5 * chunk + 5]
        for which in range(2):
            far = far_b if which else far_a
            for src, f1, f2 in ((own.at[which], 0, 0), (one.at[which], 1, 0), (three.at[which], 0, 1), (far.at[0], 1, 1)):
                x1, x2 = a1 ^ f1, a2 ^ f2
                q = 2 * x2 + x1 if which else 2 * x1 + x2
                p = 8 * chunk + 4 * which + q
                for h in range(2):
                    part = src[128 * h : 128 * h + 128, :] + spread(fix_ref[2 * p + h], ends)
                    out_ref[p, 8 * h : 8 * h + 8] = part.reshape(8, 16, 128)


def level_rounds(n):
    edges = set()
    for b in range(n):
        edges.add(((b + 1) % n, b))
        if b:
            s = b & -b
            edges.add((b - s, b))
            edges.add(((b + s) % n, b))
    out = {}
    for src, dst in edges:
        out.setdefault(src, []).append(dst)
    rounds = []
    for src in sorted(out, key=lambda k: (-len(out[k]), k)):
        for dst in sorted(out[src]):
            for r in rounds:
                if all(s != src and d != dst for s, d in r):
                    r.append((src, dst))
                    break
            else:
                rounds.append([(src, dst)])
    table = np.zeros((2, n, len(rounds)), np.float32)
    for k, r in enumerate(rounds):
        for src, dst in r:
            if src == (dst + 1) % n:
                table[0, dst, k] = 1.0
            if dst:
                s = dst & -dst
                table[1, dst, k] -= 0.5 * ((src == dst - s) + (src == (dst + s) % n))
    return rounds, table


def surplus_matrix():
    m = np.eye(128, dtype=np.float32)
    for j in range(1, 128):
        s = j & -j
        m[j - s, j] -= 0.5
        if j + s < 128:
            m[j + s, j] -= 0.5
    return m


def local(initial, levels, weights, velocity, diffusivity):
    near = [(i, i ^ 1) for i in range(4)]
    mirror = [(i, 3 - i) for i in range(4)]
    pair = [(0, 1), (1, 0)]
    n = lax.axis_size(BRICK)
    up = [(i, (i + 1) % n) for i in range(n)]
    down = [(i, (i - 1) % n) for i in range(n)]
    x = initial[0]
    pos = jnp.stack([lax.axis_index("y"), lax.axis_index(BRICK)]).astype(jnp.int32)
    layers = jax.ShapeDtypeStruct((2, 16, 256), F32)
    params = compiler_params()

    lo, hi = pl.pallas_call(ends_kernel, out_shape=(layers, layers), in_specs=[VM], out_specs=(VM, VM), compiler_params=params)(x)
    left = lax.ppermute(hi, BRICK, up)
    right = lax.ppermute(lo, BRICK, down)
    u = pl.pallas_call(
        first_kernel,
        out_shape=jax.ShapeDtypeStruct(x.shape, F32),
        in_specs=[SM] * 3 + [VM],
        out_specs=VM,
        compiler_params=params,
        cost_estimate=pl.CostEstimate(flops=10000000, bytes_accessed=4 << 20, transcendentals=0),
    )(levels, velocity, diffusivity, x)
    half = jax.ShapeDtypeStruct((2, 256, 128), F32)
    outs = pl.pallas_call(
        second_kernel,
        out_shape=(half,) * 8 + (jax.ShapeDtypeStruct((16, 256), F32),),
        in_specs=[SM] * 5 + [VM] * 5,
        out_specs=(VM,) * 9,
        scratch_shapes=[pltpu.VMEM((16, 16, 16, 128), F32), pltpu.VMEM((2, 32, 8, 128), F32)],
        compiler_params=params,
    )(levels, velocity, diffusivity, weights, pos, u, lo, hi, left, right)
    first = outs[8]

    steps = []
    for c in range(2):
        send_a, keep_a, send_b, keep_b = outs[4 * c : 4 * c + 4]
        steps.append((keep_a, keep_b, lax.ppermute(send_a, "y", near), lax.ppermute(send_b, "y", mirror)))
    pieces = []
    for keep_a, keep_b, got_a, got_b in steps:
        more_a = lax.ppermute(keep_a[0] + got_a[0], "y", mirror)
        more_b = lax.ppermute(keep_b[0] + got_b[0], "y", near)
        mine = jnp.stack([keep_a[1] + got_a[1] + more_a, keep_b[1] + got_b[1] + more_b])
        other = lax.ppermute(mine, "zh", pair)
        own = pl.pallas_call(
            surplus_kernel, out_shape=half, in_specs=[VM] * 3, out_specs=VM, compiler_params=params
        )(mine, other, jnp.asarray(surplus_matrix()))
        one = lax.ppermute(own, "y", near)
        three = lax.ppermute(own, "y", mirror)
        far_a = lax.ppermute(three[0:1], "y", near)
        far_b = lax.ppermute(one[1:2], "y", mirror)
        pieces += [own, one, three, far_a, far_b]

    first = first + lax.ppermute(first, "y", near)
    first = first + lax.ppermute(first, "y", mirror)
    first = first + lax.ppermute(first, "zh", pair)
    rounds, table = level_rounds(n)
    got = [lax.ppermute(first, BRICK, r) for r in rounds]
    return pl.pallas_call(
        functools.partial(last_kernel, len(rounds)),
        out_shape=jax.ShapeDtypeStruct((16, 16, 16, 128), F32),
        in_specs=[SM] * 2 + [VM] * (len(rounds) + len(pieces)),
        out_specs=VM,
        scratch_shapes=[pltpu.VMEM((32, 8, 128), F32)],
        compiler_params=params,
    )(pos, jnp.asarray(table), *got, *pieces)


def solution(mesh):
    wide = Mesh(mesh.devices.reshape(2, 4, 4, 4, 2), ("zh", "y", "x", "zl", "core"))
    comp = ("zh", "y")
    return jax.shard_map(
        local,
        mesh=wide,
        in_specs=(P(comp, None, None, None, BRICK), P(comp, None), P(comp), P(), P()),
        out_specs=P(None, None, None, BRICK),
        check_vma=False,
    )
```

```python
import functools
import jax
import jax.numpy as jnp
import numpy as np
from jax import lax
from jax.experimental import pallas as pl
from jax.experimental.pallas import tpu as pltpu
from jax.sharding import Mesh, PartitionSpec as P

cfl_limit = 0.9
BRICK = ("x", "zl", "core")
VM = pl.BlockSpec(memory_space=pltpu.VMEM)
SM = pl.BlockSpec(memory_space=pltpu.SMEM)
F32 = jnp.float32


def grant(mib):
    return pltpu.CompilerParams(vmem_limit_bytes=mib * 1024 * 1024)


def factors(lev, vel, dif):
    inv = [jnp.left_shift(1, lev[0, d]).astype(F32) for d in range(4)]
    total = sum(vel[d] * inv[d] + 2.0 * dif[d] * inv[d] * inv[d] for d in range(4))
    delta = cfl_limit / jnp.full((1, 128), total, F32)
    adv = [delta * (vel[d] * inv[d]) for d in range(4)]
    dfs = [delta * (dif[d] * inv[d] * inv[d]) for d in range(4)]
    center = 1.0 - sum(adv[d] + 2.0 * dfs[d] for d in range(4))
    return center, [adv[d] + dfs[d] for d in range(4)], dfs


def lane_id(shape):
    return lax.broadcasted_iota(jnp.int32, shape, len(shape) - 1)


def step_row(ref, p, i, fac):
    center, lo, hi = fac
    before, after = lax.rem(p + 15, 16), lax.rem(p + 1, 16)
    u = ref[p, i]
    out = center * u + lo[0] * ref[before, i] + hi[0] * ref[after, i]
    out = out + lo[1] * ref[p, (i + 15) % 16] + hi[1] * ref[p, (i + 1) % 16]
    out = out + lo[2] * pltpu.roll(u, 1, 0) + hi[2] * pltpu.roll(u, 15, 0)
    return out + lo[3] * pltpu.roll(u, 1, 1) + hi[3] * pltpu.roll(u, 127, 1)


def take_slot(packed_ref, slot, out_ref, at):
    for b in range(2):
        for h in range(2):
            out_ref[at, 8 * b : 8 * b + 8, 128 * h : 128 * h + 128] = packed_ref[b, pl.ds(8 * h + slot, 8, stride=16), :]


def put_slot(packed_ref, slot, value):
    for b in range(2):
        for h in range(2):
            packed_ref[b, pl.ds(8 * h + slot, 8, stride=16), :] = value[8 * b : 8 * b + 8, 128 * h : 128 * h + 128]


def ends_kernel(x_ref, full_ref, lo_ref, hi_ref, mid_ref, packed_ref, sems):
    lane = lane_id((128, 128))
    copies = [pltpu.make_async_copy(x_ref.at[pl.ds(4 * k, 4)], full_ref.at[pl.ds(4 * k, 4)], sems.at[k]) for k in range(4)]
    for copy in copies:
        copy.start()
    for b in range(2):
        acc = jnp.zeros((128, 128), F32)
        for c in range(16):
            if c % 8 == 0:
                copies[2 * b + c // 8].wait()
            block = full_ref[8 * b + c // 2, 8 * (c % 2) : 8 * (c % 2) + 8].reshape(128, 128)
            acc = jnp.where(lax.shift_right_logical(lane, 3) == c, pltpu.roll(block, (4 + 8 * c) % 128, 1), acc)
        packed_ref[b] = acc.T
    for slot, (out_ref, at) in enumerate(
        ((mid_ref, 0), (mid_ref, 1), (hi_ref, 0), (hi_ref, 1), (lo_ref, 0), (lo_ref, 1), (lo_ref, 2), (mid_ref, 2))
    ):
        take_slot(packed_ref, slot, out_ref, at)


def first_kernel(lev, vel, dif, x_ref, u_ref):
    fac = factors(lev, vel, dif)

    def plane(p, _):
        for i in range(16):
            u_ref[p, i] = step_row(x_ref, p, i, fac)
        return 0

    lax.fori_loop(0, 16, plane, 0)


def layer_step(u, below, above, center, lo, hi):
    def wide(v):
        return jnp.concatenate([v, v], axis=1)

    lane = lane_id((16, 256)) & 15
    out = wide(center) * u + wide(lo[0]) * pltpu.roll(u, 1, 0) + wide(hi[0]) * pltpu.roll(u, 15, 0)
    out = out + wide(lo[1]) * pltpu.roll(u, 16, 1) + wide(hi[1]) * pltpu.roll(u, 240, 1)
    down = jnp.where(lane == 0, pltpu.roll(u, 241, 1), pltpu.roll(u, 1, 1))
    up = jnp.where(lane == 15, pltpu.roll(u, 15, 1), pltpu.roll(u, 255, 1))
    out = out + wide(lo[2]) * down + wide(hi[2]) * up
    return out + wide(lo[3]) * below + wide(hi[3]) * above


def layers_kernel(lev, vel, dif, wgt, pos, lo_ref, hi_ref, mid_ref, left_ref, right_ref, edge_ref, shared_ref, packed_ref):
    fac = factors(lev, vel, dif)
    weight = wgt[0].astype(F32)

    def step(seq):
        return [layer_step(seq[k], seq[k - 1], seq[k + 1], *fac) for k in range(1, len(seq) - 1)]

    low = step(step([left_ref[0], left_ref[1], lo_ref[0], lo_ref[1], lo_ref[2], mid_ref[2]]))
    high = step(step([mid_ref[0], mid_ref[1], hi_ref[0], hi_ref[1], right_ref[0], right_ref[1], right_ref[2]]))
    packed_ref[...] = jnp.zeros_like(packed_ref)
    for slot, value in enumerate((high[0], high[1], low[0], low[1], high[2])):
        put_slot(packed_ref, slot, weight * value)
    edge_ref[...] = packed_ref[...].reshape(256, 128)
    shared = jnp.where((pos[1] & 1) == 1, weight * high[2], weight * low[0])
    shared_ref[0:16] = shared[:, :128]
    shared_ref[16:32] = shared[:, 128:]


def partners(y):
    return y, y ^ 1, 3 - y, y ^ 2


def second_kernel(chunk, lev, vel, dif, wgt, pos, u_ref, edge_ref, shared_ref, *outs):
    fac = factors(lev, vel, dif)
    weight = wgt[0].astype(F32)
    for target, out_ref in zip(partners(pos[0]), outs):

        def body(r, _, target=target, out_ref=out_ref):
            p = 4 * target + 2 * chunk + r
            base = pl.multiple_of(272 * r, 16)
            for i in range(16):
                out_ref[pl.ds(base + 16 * i, 16), :] = weight * step_row(u_ref, p, i, fac)
            out_ref[pl.ds(base + 256, 16), :] = edge_ref[pl.ds(pl.multiple_of(16 * p, 16), 16), :]
            return 0

        lax.fori_loop(0, 2, body, 0)
        if out_ref.shape[0] > 544:
            out_ref[544:] = shared_ref[...]


def surplus_rows(a_ref, b_ref, mat_ref, o_ref, packed_ref):
    packed_ref[...] = jnp.zeros_like(packed_ref)
    for n in range(2):
        at = slice(272 * n + 256, 272 * n + 272)
        packed_ref[16 * n : 16 * n + 16] = a_ref[at] + b_ref[at]
    turned = packed_ref[...].T
    lane = lane_id((1, 128))
    edge = (lane < 2) | (lane > 125)
    ramp = lane.astype(F32) * (1.0 / 128.0)
    for n in range(2):
        for h in range(2):
            at = slice(272 * n + 128 * h, 272 * n + 128 * h + 128)
            ends = pltpu.roll(turned, 126 - 8 * (2 * n + h), 1)
            full = jnp.where(edge, ends, a_ref[at] + b_ref[at]) - ramp * ends[:, 2:3]
            o_ref[256 * n + 128 * h : 256 * n + 128 * h + 128] = jnp.dot(
                full, mat_ref[...], precision=lax.Precision.HIGHEST, preferred_element_type=F32
            )


def surplus_kernel(a_ref, b_ref, mat_ref, o_ref, shared_ref, packed_ref):
    shared_ref[...] = a_ref[544:] + b_ref[544:]
    surplus_rows(a_ref, b_ref, mat_ref, o_ref, packed_ref)


def surplus_fix_kernel(pos, table, a_ref, b_ref, mat_ref, shared_ref, *rest):
    got, (o_ref, packed_ref) = rest[:-2], rest[-2:]
    surplus_rows(a_ref, b_ref, mat_ref, o_ref, packed_ref)
    at = 32 * pos[0] + pos[1]
    fix = table[len(got), at] * shared_ref[...]
    for k, ref in enumerate(got):
        fix = fix + table[k, at] * ref[...]
    o_ref[512:] = fix


def last_kernel(pos, *refs):
    pieces, (out_ref, packed_ref, turned_ref) = refs[:-3], refs[-3:]
    fix = sum(ref[512:] for ref in pieces[4:])
    for b in range(2):
        for h in range(2):
            packed_ref[b, pl.ds(8 * h, 8, stride=16), :] = fix[16 * h + 8 * b : 16 * h + 8 * b + 8]
        turned_ref[b] = packed_ref[b].T
    first = lane_id((1, 128)) == 0
    for chunk in range(2):
        for target, src in zip(partners(pos[0]), pieces[4 * chunk : 4 * chunk + 4]):
            turned = turned_ref[lax.shift_right_logical(target, 1)]
            for r in range(2):
                p = 4 * target + 2 * chunk + r
                for h in range(2):
                    k = (2 * p + h) & 15
                    fixed = pltpu.roll(turned, (128 - 8 * k) & 127, 1)
                    part = src[256 * r + 128 * h : 256 * r + 128 * h + 128, :] + jnp.where(first, fixed, 0.0)
                    out_ref[p, 8 * h : 8 * h + 8] = part.reshape(8, 16, 128)


def surplus_matrix():
    m = np.eye(128, dtype=np.float32)
    for j in range(1, 128):
        s = j & -j
        m[j - s, j] -= 0.5
        if j + s < 128:
            m[j + s, j] -= 0.5
    return m


def after(value, *others):
    return lax.optimization_barrier((value,) + others)[0]


def tree_edges(n, replicas):
    edges = []
    for b in range(1, n):
        s = b & -b
        if s == 1:
            edges.append((b - 1, b, -0.5))
        elif (b + s) % n == b - s:
            edges.append((b - s, b, -1.0))
        else:
            edges += [(b - s, b, -0.5), ((b + s) % n, b, -0.5)]
    degree = [sum(e[0] == b for e in edges) for b in range(n)]
    colours = max(degree + [sum(e[1] == b for e in edges) for b in range(n)])
    colours = -(-colours // replicas) * replicas
    out, into, used = {}, {}, {}

    def swap_path(v, side, c, d):
        path, here, colour = [], (side, v), c
        while True:
            key = (out if here[0] == 0 else into).get((here[1], colour))
            if key is None:
                break
            path.append((key, colour))
            here = (1 - here[0], key[1] if here[0] == 0 else key[0])
            colour = d if colour == c else c
        for key, col in path:
            del out[(key[0], col)], into[(key[1], col)]
        for key, col in path:
            new = d if col == c else c
            out[(key[0], new)] = into[(key[1], new)] = key
            used[key] = new

    for src, dst, _ in sorted(edges, key=lambda e: (-degree[e[0]], e)):
        free_src = [c for c in range(colours) if (src, c) not in out]
        free_dst = [c for c in range(colours) if (dst, c) not in into]
        both = [c for c in free_src if c in free_dst]
        colour = both[0] if both else free_src[0]
        if not both:
            swap_path(dst, 1, colour, free_dst[0])
        out[(src, colour)] = into[(dst, colour)] = (src, dst)
        used[(src, dst)] = colour
    count = colours // replicas
    rounds = [[] for _ in range(count)]
    table = np.zeros((count + 1, replicas * n), np.float32)
    for src, dst, factor in edges:
        k, y = divmod(used[(src, dst)], replicas)
        rounds[k].append((y * n + src, y * n + dst))
        table[k, y * n + dst] = factor
    table[count, 1:n:2] = -0.5
    return rounds, table


def local(initial, levels, weights, velocity, diffusivity):
    others = [[(i, partners(i)[k]) for i in range(4)] for k in (1, 2, 3)]
    pair = [(0, 1), (1, 0)]
    n = lax.axis_size(BRICK)
    up = [(i, (i + 1) % n) for i in range(n)]
    down = [(i, (i - 1) % n) for i in range(n)]
    x = initial[0]
    pos = jnp.stack([lax.axis_index("y"), lax.axis_index(BRICK)]).astype(jnp.int32)
    scalars = (levels, velocity, diffusivity, weights, pos)

    def struct(*shape):
        return jax.ShapeDtypeStruct(shape, F32)

    full, lo, hi, mid = pl.pallas_call(
        ends_kernel,
        out_shape=(struct(*x.shape), struct(3, 16, 256), struct(2, 16, 256), struct(3, 16, 256)),
        in_specs=[pl.BlockSpec(memory_space=pltpu.HBM)],
        out_specs=(VM,) * 4,
        scratch_shapes=[pltpu.VMEM((2, 128, 128), F32), pltpu.SemaphoreType.DMA((4,))],
        compiler_params=grant(4),
    )(x)
    left = lax.ppermute(hi, BRICK, up)
    right = lax.ppermute(lo, BRICK, down)
    cost = pl.CostEstimate(flops=10000000, bytes_accessed=4 << 20, transcendentals=0)
    u = pl.pallas_call(
        first_kernel,
        out_shape=struct(*x.shape),
        in_specs=[SM] * 3 + [VM],
        out_specs=VM,
        compiler_params=grant(6),
        cost_estimate=cost,
    )(levels, velocity, diffusivity, full)
    left, right = after((left, right), u)
    edges, shared = pl.pallas_call(
        layers_kernel,
        out_shape=(struct(256, 128), struct(32, 128)),
        scratch_shapes=[pltpu.VMEM((2, 128, 128), F32)],
        in_specs=[SM] * 5 + [VM] * 5,
        out_specs=(VM,) * 2,
        compiler_params=grant(2),
    )(*scalars, lo, hi, mid, left, right)

    def second(c, value):
        return pl.pallas_call(
            functools.partial(second_kernel, c),
            out_shape=(struct(544 if c else 576, 128),) * 4,
            in_specs=[SM] * 5 + [VM] * 3,
            out_specs=(VM,) * 4,
            compiler_params=grant(5),
            cost_estimate=cost,
        )(*scalars, value, edges, shared)

    def to_others(values):
        return [lax.ppermute(value, "y", perm) for value, perm in zip(values, others)]

    matrix = jnp.asarray(surplus_matrix())
    rounds, table = tree_edges(n, 4)
    parts0 = second(0, u)
    got0 = to_others(parts0[1:])
    parts1 = second(1, after(u, parts0[0]))
    got1 = to_others(after(parts1[1:], got0[0]))
    summed0 = parts0[0] + got0[0] + got0[1] + got0[2]
    other0 = lax.ppermute(summed0, "zh", pair)
    summed1 = parts1[0] + got1[0] + got1[1] + got1[2]
    other1 = lax.ppermute(summed1, "zh", pair)
    own0, shared = pl.pallas_call(
        surplus_kernel,
        out_shape=(struct(512, 128), struct(32, 128)),
        in_specs=[VM] * 3,
        out_specs=(VM,) * 2,
        scratch_shapes=[pltpu.VMEM((128, 128), F32)],
        compiler_params=grant(2),
    )(summed0, after(other0, summed1), matrix)
    pieces0 = [own0] + to_others([own0] * 3)
    got = [lax.ppermute(shared, ("y",) + BRICK, r) for r in rounds]
    own1 = pl.pallas_call(
        surplus_fix_kernel,
        out_shape=struct(544, 128),
        in_specs=[SM] * 2 + [VM] * (4 + len(got)),
        out_specs=VM,
        scratch_shapes=[pltpu.VMEM((128, 128), F32)],
        compiler_params=grant(2),
    )(pos, jnp.asarray(table), summed1, after(other1, *pieces0), matrix, shared, *got)
    pieces = pieces0 + [own1] + to_others([own1] * 3)

    return pl.pallas_call(
        last_kernel,
        out_shape=struct(16, 16, 16, 128),
        in_specs=[SM] + [VM] * len(pieces),
        out_specs=VM,
        scratch_shapes=[pltpu.VMEM((2, 128, 128), F32)] * 2,
        compiler_params=grant(8),
    )(pos, *pieces)


def solution(mesh):
    wide = Mesh(mesh.devices.reshape(2, 4, 4, 4, 2), ("zh", "y", "x", "zl", "core"))
    comp = ("zh", "y")
    return jax.shard_map(
        local,
        mesh=wide,
        in_specs=(P(comp, None, None, None, BRICK), P(comp, None), P(comp), P(), P()),
        out_specs=P(None, None, None, BRICK),
        check_vma=False,
    )
```

```python
import functools
import jax
import jax.numpy as jnp
import numpy as np
from jax import lax
from jax.experimental import pallas as pl
from jax.experimental.pallas import tpu as pltpu
from jax.sharding import Mesh, PartitionSpec as P

cfl_limit = 0.9
BRICK = ("x", "zl", "core")
VM = pl.BlockSpec(memory_space=pltpu.VMEM)
SM = pl.BlockSpec(memory_space=pltpu.SMEM)
F32 = jnp.float32
CHUNKS = ((0, 1), (1, 2), (3, 1))


def grant(mib):
    return pltpu.CompilerParams(vmem_limit_bytes=mib * 1024 * 1024)


def factors(lev, vel, dif):
    inv = [jnp.left_shift(1, lev[0, d]).astype(F32) for d in range(4)]
    total = sum(vel[d] * inv[d] + 2.0 * dif[d] * inv[d] * inv[d] for d in range(4))
    delta = cfl_limit / jnp.full((1, 128), total, F32)
    adv = [delta * (vel[d] * inv[d]) for d in range(4)]
    dfs = [delta * (dif[d] * inv[d] * inv[d]) for d in range(4)]
    center = 1.0 - sum(adv[d] + 2.0 * dfs[d] for d in range(4))
    return center, [adv[d] + dfs[d] for d in range(4)], dfs


def lane_id(shape):
    return lax.broadcasted_iota(jnp.int32, shape, len(shape) - 1)


def step_row(ref, p, i, fac):
    center, lo, hi = fac
    before, after = lax.rem(p + 15, 16), lax.rem(p + 1, 16)
    u = ref[p, i]
    out = center * u + lo[0] * ref[before, i] + hi[0] * ref[after, i]
    out = out + lo[1] * ref[p, (i + 15) % 16] + hi[1] * ref[p, (i + 1) % 16]
    out = out + lo[2] * pltpu.roll(u, 1, 0) + hi[2] * pltpu.roll(u, 15, 0)
    return out + lo[3] * pltpu.roll(u, 1, 1) + hi[3] * pltpu.roll(u, 127, 1)


def take_slot(packed_ref, slot, out_ref, at):
    for b in range(2):
        for h in range(2):
            out_ref[at, 8 * b : 8 * b + 8, 128 * h : 128 * h + 128] = packed_ref[b, pl.ds(8 * h + slot, 8, stride=16), :]


def put_slot(packed_ref, slot, value):
    for b in range(2):
        for h in range(2):
            packed_ref[b, pl.ds(8 * h + slot, 8, stride=16), :] = value[8 * b : 8 * b + 8, 128 * h : 128 * h + 128]


def ends_kernel(x_ref, lo_ref, hi_ref, mid_ref, packed_ref):
    lane = lane_id((128, 128))
    for b in range(2):
        acc = jnp.zeros((128, 128), F32)
        for c in range(16):
            block = x_ref[8 * b + c // 2, 8 * (c % 2) : 8 * (c % 2) + 8].reshape(128, 128)
            acc = jnp.where(lax.shift_right_logical(lane, 3) == c, pltpu.roll(block, (4 + 8 * c) % 128, 1), acc)
        packed_ref[b] = acc.T
    for slot, (out_ref, at) in enumerate(
        ((mid_ref, 0), (mid_ref, 1), (hi_ref, 0), (hi_ref, 1), (lo_ref, 0), (lo_ref, 1), (lo_ref, 2), (mid_ref, 2))
    ):
        take_slot(packed_ref, slot, out_ref, at)


def first_kernel(lev, vel, dif, x_ref, u_ref):
    fac = factors(lev, vel, dif)

    def plane(p, _):
        for i in range(16):
            u_ref[p, i] = step_row(x_ref, p, i, fac)
        return 0

    lax.fori_loop(0, 16, plane, 0)


def layer_step(u, below, above, center, lo, hi):
    def wide(v):
        return jnp.concatenate([v, v], axis=1)

    lane = lane_id((16, 256)) & 15
    out = wide(center) * u + wide(lo[0]) * pltpu.roll(u, 1, 0) + wide(hi[0]) * pltpu.roll(u, 15, 0)
    out = out + wide(lo[1]) * pltpu.roll(u, 16, 1) + wide(hi[1]) * pltpu.roll(u, 240, 1)
    down = jnp.where(lane == 0, pltpu.roll(u, 241, 1), pltpu.roll(u, 1, 1))
    up = jnp.where(lane == 15, pltpu.roll(u, 15, 1), pltpu.roll(u, 255, 1))
    out = out + wide(lo[2]) * down + wide(hi[2]) * up
    return out + wide(lo[3]) * below + wide(hi[3]) * above


def layers_kernel(lev, vel, dif, wgt, pos, lo_ref, hi_ref, mid_ref, left_ref, right_ref, edge_ref, shared_ref, packed_ref):
    fac = factors(lev, vel, dif)
    weight = wgt[0].astype(F32)

    def step(seq):
        return [layer_step(seq[k], seq[k - 1], seq[k + 1], *fac) for k in range(1, len(seq) - 1)]

    low = step(step([left_ref[0], left_ref[1], lo_ref[0], lo_ref[1], lo_ref[2], mid_ref[2]]))
    high = step(step([mid_ref[0], mid_ref[1], hi_ref[0], hi_ref[1], right_ref[0], right_ref[1], right_ref[2]]))
    packed_ref[...] = jnp.zeros_like(packed_ref)
    for slot, value in enumerate((high[0], high[1], low[0], low[1], high[2])):
        put_slot(packed_ref, slot, weight * value)
    edge_ref[...] = packed_ref[...].reshape(256, 128)
    shared = jnp.where((pos[1] & 1) == 1, weight * high[2], weight * low[0])
    shared_ref[0:16] = shared[:, :128]
    shared_ref[16:32] = shared[:, 128:]


def partners(y):
    return y, y ^ 1, 3 - y, y ^ 2


def second_kernel(chunk, lev, vel, dif, wgt, pos, u_ref, edge_ref, shared_ref, *outs):
    fac = factors(lev, vel, dif)
    weight = wgt[0].astype(F32)
    for target, out_ref in zip(partners(pos[0]), outs):

        def body(r, _, target=target, out_ref=out_ref):
            p = 4 * target + CHUNKS[chunk][0] + r
            base = pl.multiple_of(272 * r, 16)
            for i in range(16):
                out_ref[pl.ds(base + 16 * i, 16), :] = weight * step_row(u_ref, p, i, fac)
            out_ref[pl.ds(base + 256, 16), :] = edge_ref[pl.ds(pl.multiple_of(16 * p, 16), 16), :]
            return 0

        lax.fori_loop(0, CHUNKS[chunk][1], body, 0)
        if chunk == 0:
            out_ref[272 * CHUNKS[0][1] :] = shared_ref[...]


def surplus_rows(a_ref, b_ref, mat_ref, o_ref, packed_ref):
    planes = a_ref.shape[0] // 272
    packed_ref[...] = jnp.zeros_like(packed_ref)
    for n in range(planes):
        at = slice(272 * n + 256, 272 * n + 272)
        packed_ref[16 * n : 16 * n + 16] = a_ref[at] + b_ref[at]
    turned = packed_ref[...].T
    lane = lane_id((1, 128))
    edge = (lane < 2) | (lane > 125)
    ramp = lane.astype(F32) * (1.0 / 128.0)
    for n in range(planes):
        for h in range(2):
            at = slice(272 * n + 128 * h, 272 * n + 128 * h + 128)
            ends = pltpu.roll(turned, 126 - 8 * (2 * n + h), 1)
            full = jnp.where(edge, ends, a_ref[at] + b_ref[at]) - ramp * ends[:, 2:3]
            o_ref[256 * n + 128 * h : 256 * n + 128 * h + 128] = jnp.dot(
                full, mat_ref[...], precision=lax.Precision.HIGHEST, preferred_element_type=F32
            )
    return 272 * planes, 256 * planes


def surplus_kernel(a_ref, b_ref, mat_ref, o_ref, packed_ref):
    surplus_rows(a_ref, b_ref, mat_ref, o_ref, packed_ref)


def surplus_fix_kernel(pos, table, a_ref, b_ref, mat_ref, shared_ref, *rest):
    got, (o_ref, packed_ref) = rest[:-2], rest[-2:]
    _, end = surplus_rows(a_ref, b_ref, mat_ref, o_ref, packed_ref)
    at = 32 * pos[0] + pos[1]
    fix = table[len(got), at] * shared_ref[...]
    for k, ref in enumerate(got):
        fix = fix + table[k, at] * ref[...]
    o_ref[end:] = fix


def write_planes(chunks, y, pieces, turned_ref, out_ref, block_ref, sems):
    first = lane_id((1, 128)) == 0
    start, count = CHUNKS[chunks[0]][0], sum(CHUNKS[c][1] for c in chunks)
    copies = []
    for t, target in enumerate(partners(y)):
        turned = turned_ref[lax.shift_right_logical(target, 1)]
        at = 0
        for c, refs in zip(chunks, pieces):
            for r in range(CHUNKS[c][1]):
                for h in range(2):
                    k = (2 * (4 * target + start + at) + h) & 15
                    fixed = pltpu.roll(turned, (128 - 8 * k) & 127, 1)
                    part = refs[t][256 * r + 128 * h : 256 * r + 128 * h + 128, :] + jnp.where(first, fixed, 0.0)
                    block_ref[count * t + at, 8 * h : 8 * h + 8] = part.reshape(8, 16, 128)
                at += 1
        copy = pltpu.make_async_copy(
            block_ref.at[pl.ds(count * t, count)], out_ref.at[pl.ds(4 * target + start, count)], sems.at[t]
        )
        copy.start()
        copies.append(copy)
    for copy in copies:
        copy.wait()


def early_kernel(pos, *refs):
    pieces, (out_ref, turned_ref, packed_ref, block_ref, sems) = refs[:8], refs[8:]
    fix = sum(ref[256 * CHUNKS[1][1] :] for ref in pieces[4:])
    for b in range(2):
        for h in range(2):
            packed_ref[b, pl.ds(8 * h, 8, stride=16), :] = fix[16 * h + 8 * b : 16 * h + 8 * b + 8]
        turned_ref[b] = packed_ref[b].T
    write_planes((0, 1), pos[0], (pieces[:4], pieces[4:]), turned_ref, out_ref, block_ref, sems)


def last_kernel(pos, *refs):
    pieces, (turned_ref, _, out_ref, block_ref, sems) = refs[:4], refs[4:]
    write_planes((2,), pos[0], (pieces,), turned_ref, out_ref, block_ref, sems)


def surplus_matrix():
    m = np.eye(128, dtype=np.float32)
    for j in range(1, 128):
        s = j & -j
        m[j - s, j] -= 0.5
        if j + s < 128:
            m[j + s, j] -= 0.5
    return m


def after(value, *others):
    return lax.optimization_barrier((value,) + others)[0]


def tree_edges(n, replicas):
    edges = []
    for b in range(1, n):
        s = b & -b
        if s == 1:
            edges.append((b - 1, b, -0.5))
        elif (b + s) % n == b - s:
            edges.append((b - s, b, -1.0))
        else:
            edges += [(b - s, b, -0.5), ((b + s) % n, b, -0.5)]
    degree = [sum(e[0] == b for e in edges) for b in range(n)]
    colours = max(degree + [sum(e[1] == b for e in edges) for b in range(n)])
    colours = -(-colours // replicas) * replicas
    out, into, used = {}, {}, {}

    def swap_path(v, side, c, d):
        path, here, colour = [], (side, v), c
        while True:
            key = (out if here[0] == 0 else into).get((here[1], colour))
            if key is None:
                break
            path.append((key, colour))
            here = (1 - here[0], key[1] if here[0] == 0 else key[0])
            colour = d if colour == c else c
        for key, col in path:
            del out[(key[0], col)], into[(key[1], col)]
        for key, col in path:
            new = d if col == c else c
            out[(key[0], new)] = into[(key[1], new)] = key
            used[key] = new

    for src, dst, _ in sorted(edges, key=lambda e: (-degree[e[0]], e)):
        free_src = [c for c in range(colours) if (src, c) not in out]
        free_dst = [c for c in range(colours) if (dst, c) not in into]
        both = [c for c in free_src if c in free_dst]
        colour = both[0] if both else free_src[0]
        if not both:
            swap_path(dst, 1, colour, free_dst[0])
        out[(src, colour)] = into[(dst, colour)] = (src, dst)
        used[(src, dst)] = colour
    count = colours // replicas
    rounds = [[] for _ in range(count)]
    table = np.zeros((count + 1, replicas * n), np.float32)
    for src, dst, factor in edges:
        k, y = divmod(used[(src, dst)], replicas)
        rounds[k].append((y * n + src, y * n + dst))
        table[k, y * n + dst] = factor
    table[count, 1:n:2] = -0.5
    return rounds, table


def local(initial, levels, weights, velocity, diffusivity):
    others = [[(i, partners(i)[k]) for i in range(4)] for k in (1, 2, 3)]
    pair = [(0, 1), (1, 0)]
    n = lax.axis_size(BRICK)
    up = [(i, (i + 1) % n) for i in range(n)]
    down = [(i, (i - 1) % n) for i in range(n)]
    x = initial[0]
    pos = jnp.stack([lax.axis_index("y"), lax.axis_index(BRICK)]).astype(jnp.int32)
    scalars = (levels, velocity, diffusivity, weights, pos)

    def struct(*shape):
        return jax.ShapeDtypeStruct(shape, F32)

    lo, hi, mid = pl.pallas_call(
        ends_kernel,
        out_shape=(struct(3, 16, 256), struct(2, 16, 256), struct(3, 16, 256)),
        in_specs=[VM],
        out_specs=(VM,) * 3,
        scratch_shapes=[pltpu.VMEM((2, 128, 128), F32)],
        compiler_params=grant(4),
    )(x)
    left = lax.ppermute(hi, BRICK, up)
    right = lax.ppermute(lo, BRICK, down)
    cost = pl.CostEstimate(flops=10000000, bytes_accessed=4 << 20, transcendentals=0)
    u = pl.pallas_call(
        first_kernel,
        out_shape=struct(*x.shape),
        in_specs=[SM] * 3 + [VM],
        out_specs=VM,
        compiler_params=grant(6),
        cost_estimate=cost,
    )(levels, velocity, diffusivity, x)
    left, right = after((left, right), u)
    edges, shared = pl.pallas_call(
        layers_kernel,
        out_shape=(struct(256, 128), struct(32, 128)),
        scratch_shapes=[pltpu.VMEM((2, 128, 128), F32)],
        in_specs=[SM] * 5 + [VM] * 5,
        out_specs=(VM,) * 2,
        compiler_params=grant(2),
    )(*scalars, lo, hi, mid, left, right)

    def second(c, value):
        return pl.pallas_call(
            functools.partial(second_kernel, c),
            out_shape=(struct(272 * CHUNKS[c][1] + (0 if c else 32), 128),) * 4,
            in_specs=[SM] * 5 + [VM] * 3,
            out_specs=(VM,) * 4,
            compiler_params=grant(5),
            cost_estimate=cost,
        )(*scalars, value, edges, shared)

    def to_others(values):
        return [lax.ppermute(value, "y", perm) for value, perm in zip(values, others)]

    def surplus(kernel, out, *args, scalar=0):
        return pl.pallas_call(
            kernel,
            out_shape=out,
            in_specs=[SM] * scalar + [VM] * (len(args) - scalar),
            out_specs=jax.tree.map(lambda _: VM, out),
            scratch_shapes=[pltpu.VMEM((128, 128), F32)],
            compiler_params=grant(3),
        )(*args)

    matrix = jnp.asarray(surplus_matrix())
    rounds, table = tree_edges(n, 4)
    sizes = [256 * count for _, count in CHUNKS]
    value, gate, summed, partner = u, (), [], []
    for c in range(3):
        parts = second(c, value)
        value = after(u, parts[0])
        got = to_others(after(parts[1:], *gate))
        gate = (got[0],)
        summed.append(parts[0] + got[0] + got[1] + got[2])
        partner.append(lax.ppermute(summed[c], "zh", pair))
    shared = summed[0][-32:] + partner[0][-32:]
    own0 = surplus(surplus_kernel, struct(sizes[0], 128), summed[0], after(partner[0], summed[2]), matrix)
    pieces0 = [own0] + to_others([own0] * 3)
    got = [lax.ppermute(shared, ("y",) + BRICK, r) for r in rounds]
    own1 = surplus(
        surplus_fix_kernel,
        struct(sizes[1] + 32, 128),
        pos,
        jnp.asarray(table),
        summed[1],
        after(partner[1], *pieces0),
        matrix,
        shared,
        *got,
        scalar=2,
    )
    pieces1 = [own1] + to_others([own1] * 3)
    own2 = surplus(surplus_kernel, struct(sizes[2], 128), summed[2], after(partner[2], own1), matrix)
    pieces2 = [own2] + to_others([own2] * 3)

    hbm = pl.BlockSpec(memory_space=pl.ANY)
    whole = struct(16, 16, 16, 128)
    early = CHUNKS[0][1] + CHUNKS[1][1]
    out, turned = pl.pallas_call(
        early_kernel,
        out_shape=(whole, struct(2, 128, 128)),
        in_specs=[SM] + [VM] * 8,
        out_specs=(hbm, VM),
        scratch_shapes=[
            pltpu.VMEM((2, 128, 128), F32),
            pltpu.VMEM((4 * early, 16, 16, 128), F32),
            pltpu.SemaphoreType.DMA((4,)),
        ],
        compiler_params=grant(6),
        cost_estimate=cost,
    )(pos, *pieces0, *pieces1)
    return pl.pallas_call(
        last_kernel,
        out_shape=whole,
        in_specs=[SM] + [VM] * 5 + [hbm],
        out_specs=hbm,
        scratch_shapes=[pltpu.VMEM((4 * CHUNKS[2][1], 16, 16, 128), F32), pltpu.SemaphoreType.DMA((4,))],
        input_output_aliases={6: 0},
        compiler_params=grant(4),
    )(pos, *pieces2, turned, out)


def solution(mesh):
    wide = Mesh(mesh.devices.reshape(2, 4, 4, 4, 2), ("zh", "y", "x", "zl", "core"))
    comp = ("zh", "y")
    return jax.shard_map(
        local,
        mesh=wide,
        in_specs=(P(comp, None, None, None, BRICK), P(comp, None), P(comp), P(), P()),
        out_specs=P(None, None, None, BRICK),
        check_vma=False,
    )
```

```python
import functools
import jax
import jax.numpy as jnp
import numpy as np
from jax import lax
from jax.experimental import pallas as pl
from jax.experimental.pallas import tpu as pltpu
from jax.sharding import Mesh, PartitionSpec as P

cfl_limit = 0.9
BRICK = ("x", "zl", "core")
VM = pl.BlockSpec(memory_space=pltpu.VMEM)
SM = pl.BlockSpec(memory_space=pltpu.SMEM)
F32 = jnp.float32
CHUNKS = ((0, 1), (1, 1), (2, 2))


def grant(mib):
    return pltpu.CompilerParams(vmem_limit_bytes=mib * 1024 * 1024)


def factors(lev, vel, dif):
    inv = [jnp.left_shift(1, lev[0, d]).astype(F32) for d in range(4)]
    total = sum(vel[d] * inv[d] + 2.0 * dif[d] * inv[d] * inv[d] for d in range(4))
    delta = cfl_limit / jnp.full((1, 128), total, F32)
    adv = [delta * (vel[d] * inv[d]) for d in range(4)]
    dfs = [delta * (dif[d] * inv[d] * inv[d]) for d in range(4)]
    center = 1.0 - sum(adv[d] + 2.0 * dfs[d] for d in range(4))
    return center, [adv[d] + dfs[d] for d in range(4)], dfs


def lane_id(shape):
    return lax.broadcasted_iota(jnp.int32, shape, len(shape) - 1)


def step_row(ref, p, i, fac):
    center, lo, hi = fac
    before, after = lax.rem(p + 15, 16), lax.rem(p + 1, 16)
    u = ref[p, i]
    out = center * u + lo[0] * ref[before, i] + hi[0] * ref[after, i]
    out = out + lo[1] * ref[p, (i + 15) % 16] + hi[1] * ref[p, (i + 1) % 16]
    out = out + lo[2] * pltpu.roll(u, 1, 0) + hi[2] * pltpu.roll(u, 15, 0)
    return out + lo[3] * pltpu.roll(u, 1, 1) + hi[3] * pltpu.roll(u, 127, 1)


def take_slot(packed_ref, slot, out_ref, at):
    for b in range(2):
        for h in range(2):
            out_ref[at, 8 * b : 8 * b + 8, 128 * h : 128 * h + 128] = packed_ref[b, pl.ds(8 * h + slot, 8, stride=16), :]


def put_slot(packed_ref, slot, value):
    for b in range(2):
        for h in range(2):
            packed_ref[b, pl.ds(8 * h + slot, 8, stride=16), :] = value[8 * b : 8 * b + 8, 128 * h : 128 * h + 128]


def ends_kernel(x_ref, lo_ref, hi_ref, mid_ref, packed_ref):
    lane = lane_id((128, 128))
    for b in range(2):
        acc = jnp.zeros((128, 128), F32)
        for c in range(16):
            block = x_ref[8 * b + c // 2, 8 * (c % 2) : 8 * (c % 2) + 8].reshape(128, 128)
            acc = jnp.where(lax.shift_right_logical(lane, 3) == c, pltpu.roll(block, (4 + 8 * c) % 128, 1), acc)
        packed_ref[b] = acc.T
    for slot, (out_ref, at) in enumerate(
        ((mid_ref, 0), (mid_ref, 1), (hi_ref, 0), (hi_ref, 1), (lo_ref, 0), (lo_ref, 1), (lo_ref, 2), (mid_ref, 2))
    ):
        take_slot(packed_ref, slot, out_ref, at)


def first_kernel(lev, vel, dif, x_ref, u_ref):
    fac = factors(lev, vel, dif)

    def plane(p, _):
        for i in range(16):
            u_ref[p, i] = step_row(x_ref, p, i, fac)
        return 0

    lax.fori_loop(0, 16, plane, 0)


def layer_step(u, below, above, center, lo, hi):
    def wide(v):
        return jnp.concatenate([v, v], axis=1)

    lane = lane_id((16, 256)) & 15
    out = wide(center) * u + wide(lo[0]) * pltpu.roll(u, 1, 0) + wide(hi[0]) * pltpu.roll(u, 15, 0)
    out = out + wide(lo[1]) * pltpu.roll(u, 16, 1) + wide(hi[1]) * pltpu.roll(u, 240, 1)
    down = jnp.where(lane == 0, pltpu.roll(u, 241, 1), pltpu.roll(u, 1, 1))
    up = jnp.where(lane == 15, pltpu.roll(u, 15, 1), pltpu.roll(u, 255, 1))
    out = out + wide(lo[2]) * down + wide(hi[2]) * up
    return out + wide(lo[3]) * below + wide(hi[3]) * above


def layers_kernel(lev, vel, dif, wgt, pos, lo_ref, hi_ref, mid_ref, left_ref, right_ref, edge_ref, shared_ref, packed_ref):
    fac = factors(lev, vel, dif)
    weight = wgt[0].astype(F32)

    def step(seq):
        return [layer_step(seq[k], seq[k - 1], seq[k + 1], *fac) for k in range(1, len(seq) - 1)]

    low = step(step([left_ref[0], left_ref[1], lo_ref[0], lo_ref[1], lo_ref[2], mid_ref[2]]))
    high = step(step([mid_ref[0], mid_ref[1], hi_ref[0], hi_ref[1], right_ref[0], right_ref[1], right_ref[2]]))
    packed_ref[...] = jnp.zeros_like(packed_ref)
    for slot, value in enumerate((high[0], high[1], low[0], low[1], high[2])):
        put_slot(packed_ref, slot, weight * value)
    edge_ref[...] = packed_ref[...].reshape(256, 128)
    shared = jnp.where((pos[1] & 1) == 1, weight * high[2], weight * low[0])
    shared_ref[0:16] = shared[:, :128]
    shared_ref[16:32] = shared[:, 128:]


def partners(y):
    return y, y ^ 1, 3 - y, y ^ 2


def second_kernel(chunk, lev, vel, dif, wgt, pos, u_ref, edge_ref, shared_ref, *outs):
    fac = factors(lev, vel, dif)
    weight = wgt[0].astype(F32)
    for target, out_ref in zip(partners(pos[0]), outs):

        def body(r, _, target=target, out_ref=out_ref):
            p = 4 * target + CHUNKS[chunk][0] + r
            base = pl.multiple_of(272 * r, 16)
            for i in range(16):
                out_ref[pl.ds(base + 16 * i, 16), :] = weight * step_row(u_ref, p, i, fac)
            out_ref[pl.ds(base + 256, 16), :] = edge_ref[pl.ds(pl.multiple_of(16 * p, 16), 16), :]
            return 0

        lax.fori_loop(0, CHUNKS[chunk][1], body, 0)
        if chunk == 0:
            out_ref[272 * CHUNKS[0][1] :] = shared_ref[...]


def surplus_rows(planes, a_ref, b_ref, mat_ref, o_ref, at, packed_ref):
    for n in range(planes):
        rows = slice(272 * n + 256, 272 * n + 272)
        packed_ref[16 * n : 16 * n + 16] = a_ref[rows] + b_ref[rows]
    turned = packed_ref[...].T
    lane = lane_id((1, 128))
    edge = (lane < 2) | (lane > 125)
    ramp = lane.astype(F32) * (1.0 / 128.0)
    for n in range(planes):
        for h in range(2):
            rows = slice(272 * n + 128 * h, 272 * n + 128 * h + 128)
            ends = pltpu.roll(turned, 126 - 8 * (2 * n + h), 1)
            full = jnp.where(edge, ends, a_ref[rows] + b_ref[rows]) - ramp * ends[:, 2:3]
            o_ref[at + 256 * n + 128 * h : at + 256 * n + 128 * h + 128] = jnp.dot(
                full, mat_ref[...], precision=lax.Precision.HIGHEST, preferred_element_type=F32
            )


def surplus_pair_kernel(a_ref, b_ref, c_ref, d_ref, mat_ref, o_ref, packed_ref):
    packed_ref[...] = jnp.zeros_like(packed_ref)
    surplus_rows(1, a_ref, b_ref, mat_ref, o_ref, 0, packed_ref)
    surplus_rows(1, c_ref, d_ref, mat_ref, o_ref, 256, packed_ref)


def surplus_fix_kernel(pos, table, a_ref, b_ref, mat_ref, shared_ref, *rest):
    got, (o_ref, packed_ref) = rest[:-2], rest[-2:]
    packed_ref[...] = jnp.zeros_like(packed_ref)
    surplus_rows(2, a_ref, b_ref, mat_ref, o_ref, 0, packed_ref)
    at = 32 * pos[0] + pos[1]
    fix = table[len(got), at] * shared_ref[...]
    for k, ref in enumerate(got):
        fix = fix + table[k, at] * ref[...]
    o_ref[512:] = fix


def last_kernel(pos, *refs):
    pieces, (out_ref, packed_ref, turned_ref, block_ref, sems) = (refs[:4], refs[4:8]), refs[8:]
    fix = sum(ref[512:] for ref in pieces[1])
    for b in range(2):
        for h in range(2):
            packed_ref[b, pl.ds(8 * h, 8, stride=16), :] = fix[16 * h + 8 * b : 16 * h + 8 * b + 8]
        turned_ref[b] = packed_ref[b].T
    first = lane_id((1, 128)) == 0
    copies = []
    for half in range(2):
        for t, target in enumerate(partners(pos[0])):
            turned = turned_ref[lax.shift_right_logical(target, 1)]
            at = 8 * half + 2 * t
            for r in range(2):
                for h in range(2):
                    k = (2 * (4 * target + 2 * half + r) + h) & 15
                    fixed = pltpu.roll(turned, (128 - 8 * k) & 127, 1)
                    rows = slice(256 * r + 128 * h, 256 * r + 128 * h + 128)
                    part = pieces[half][t][rows, :] + jnp.where(first, fixed, 0.0)
                    block_ref[at + r, 8 * h : 8 * h + 8] = part.reshape(8, 16, 128)
            copy = pltpu.make_async_copy(
                block_ref.at[pl.ds(at, 2)], out_ref.at[pl.ds(4 * target + 2 * half, 2)], sems.at[4 * half + t]
            )
            copy.start()
            copies.append(copy)
    for copy in copies:
        copy.wait()


def surplus_matrix():
    m = np.eye(128, dtype=np.float32)
    for j in range(1, 128):
        s = j & -j
        m[j - s, j] -= 0.5
        if j + s < 128:
            m[j + s, j] -= 0.5
    return m


def after(value, *others):
    return lax.optimization_barrier((value,) + others)[0]


def tree_edges(n, replicas):
    edges = []
    for b in range(1, n):
        s = b & -b
        if s == 1:
            edges.append((b - 1, b, -0.5))
        elif (b + s) % n == b - s:
            edges.append((b - s, b, -1.0))
        else:
            edges += [(b - s, b, -0.5), ((b + s) % n, b, -0.5)]
    degree = [sum(e[0] == b for e in edges) for b in range(n)]
    colours = max(degree + [sum(e[1] == b for e in edges) for b in range(n)])
    colours = -(-colours // replicas) * replicas
    out, into, used = {}, {}, {}

    def swap_path(v, side, c, d):
        path, here, colour = [], (side, v), c
        while True:
            key = (out if here[0] == 0 else into).get((here[1], colour))
            if key is None:
                break
            path.append((key, colour))
            here = (1 - here[0], key[1] if here[0] == 0 else key[0])
            colour = d if colour == c else c
        for key, col in path:
            del out[(key[0], col)], into[(key[1], col)]
        for key, col in path:
            new = d if col == c else c
            out[(key[0], new)] = into[(key[1], new)] = key
            used[key] = new

    for src, dst, _ in sorted(edges, key=lambda e: (-degree[e[0]], e)):
        free_src = [c for c in range(colours) if (src, c) not in out]
        free_dst = [c for c in range(colours) if (dst, c) not in into]
        both = [c for c in free_src if c in free_dst]
        colour = both[0] if both else free_src[0]
        if not both:
            swap_path(dst, 1, colour, free_dst[0])
        out[(src, colour)] = into[(dst, colour)] = (src, dst)
        used[(src, dst)] = colour
    count = colours // replicas
    rounds = [[] for _ in range(count)]
    table = np.zeros((count + 1, replicas * n), np.float32)
    for src, dst, factor in edges:
        k, y = divmod(used[(src, dst)], replicas)
        rounds[k].append((y * n + src, y * n + dst))
        table[k, y * n + dst] = factor
    table[count, 1:n:2] = -0.5
    return rounds, table


def local(initial, levels, weights, velocity, diffusivity):
    others = [[(i, partners(i)[k]) for i in range(4)] for k in (1, 2, 3)]
    pair = [(0, 1), (1, 0)]
    n = lax.axis_size(BRICK)
    up = [(i, (i + 1) % n) for i in range(n)]
    down = [(i, (i - 1) % n) for i in range(n)]
    x = initial[0]
    pos = jnp.stack([lax.axis_index("y"), lax.axis_index(BRICK)]).astype(jnp.int32)
    scalars = (levels, velocity, diffusivity, weights, pos)

    def struct(*shape):
        return jax.ShapeDtypeStruct(shape, F32)

    lo, hi, mid = pl.pallas_call(
        ends_kernel,
        out_shape=(struct(3, 16, 256), struct(2, 16, 256), struct(3, 16, 256)),
        in_specs=[VM],
        out_specs=(VM,) * 3,
        scratch_shapes=[pltpu.VMEM((2, 128, 128), F32)],
        compiler_params=grant(4),
    )(x)
    left = lax.ppermute(hi, BRICK, up)
    right = lax.ppermute(lo, BRICK, down)
    cost = pl.CostEstimate(flops=10000000, bytes_accessed=4 << 20, transcendentals=0)
    u = pl.pallas_call(
        first_kernel,
        out_shape=struct(*x.shape),
        in_specs=[SM] * 3 + [VM],
        out_specs=VM,
        compiler_params=grant(6),
        cost_estimate=cost,
    )(levels, velocity, diffusivity, x)
    left, right = after((left, right), u)
    edges, shared = pl.pallas_call(
        layers_kernel,
        out_shape=(struct(256, 128), struct(32, 128)),
        scratch_shapes=[pltpu.VMEM((2, 128, 128), F32)],
        in_specs=[SM] * 5 + [VM] * 5,
        out_specs=(VM,) * 2,
        compiler_params=grant(2),
    )(*scalars, lo, hi, mid, left, right)

    def second(c, value):
        return pl.pallas_call(
            functools.partial(second_kernel, c),
            out_shape=(struct(272 * CHUNKS[c][1] + (0 if c else 32), 128),) * 4,
            in_specs=[SM] * 5 + [VM] * 3,
            out_specs=(VM,) * 4,
            compiler_params=grant(5),
            cost_estimate=cost,
        )(*scalars, value, edges, shared)

    def to_others(values):
        return [lax.ppermute(value, "y", perm) for value, perm in zip(values, others)]

    def surplus(kernel, out, *args, scalar=0):
        return pl.pallas_call(
            kernel,
            out_shape=out,
            in_specs=[SM] * scalar + [VM] * (len(args) - scalar),
            out_specs=jax.tree.map(lambda _: VM, out),
            scratch_shapes=[pltpu.VMEM((128, 128), F32)],
            compiler_params=grant(3),
        )(*args)

    matrix = jnp.asarray(surplus_matrix())
    rounds, table = tree_edges(n, 4)
    value, gate, summed, partner = u, (), [], []
    for c in range(3):
        parts = second(c, value)
        value = after(u, parts[0])
        got = to_others(after(parts[1:], *gate))
        gate = (got[0],)
        summed.append(parts[0] + got[0] + got[1] + got[2])
        partner.append(lax.ppermute(summed[c], "zh", pair))
    shared = summed[0][-32:] + partner[0][-32:]
    got = [lax.ppermute(shared, ("y",) + BRICK, r) for r in rounds]
    own0 = surplus(
        surplus_pair_kernel,
        struct(512, 128),
        summed[0],
        partner[0],
        summed[1],
        after(partner[1], summed[2]),
        matrix,
    )
    pieces0 = [own0] + to_others([own0] * 3)
    own1 = surplus(
        surplus_fix_kernel,
        struct(544, 128),
        pos,
        jnp.asarray(table),
        summed[2],
        after(partner[2], *pieces0),
        matrix,
        shared,
        *got,
        scalar=2,
    )
    pieces1 = [own1] + to_others([own1] * 3)
    return pl.pallas_call(
        last_kernel,
        out_shape=struct(16, 16, 16, 128),
        in_specs=[SM] + [VM] * 8,
        out_specs=pl.BlockSpec(memory_space=pl.ANY),
        scratch_shapes=[
            pltpu.VMEM((2, 128, 128), F32),
            pltpu.VMEM((2, 128, 128), F32),
            pltpu.VMEM((16, 16, 16, 128), F32),
            pltpu.SemaphoreType.DMA((8,)),
        ],
        compiler_params=grant(6),
    )(pos, *pieces0, *pieces1)


def solution(mesh):
    wide = Mesh(mesh.devices.reshape(2, 4, 4, 4, 2), ("zh", "y", "x", "zl", "core"))
    comp = ("zh", "y")
    return jax.shard_map(
        local,
        mesh=wide,
        in_specs=(P(comp, None, None, None, BRICK), P(comp, None), P(comp), P(), P()),
        out_specs=P(None, None, None, BRICK),
        check_vma=False,
    )
```

```python
import functools
import jax
import jax.numpy as jnp
import numpy as np
from jax import lax
from jax.experimental import pallas as pl
from jax.experimental.pallas import tpu as pltpu
from jax.sharding import Mesh, PartitionSpec as P

cfl_limit = 0.9
BRICK = ("x", "zl", "core")
VM = pl.BlockSpec(memory_space=pltpu.VMEM)
SM = pl.BlockSpec(memory_space=pltpu.SMEM)
F32 = jnp.float32
CHUNKS = ((0, 1), (1, 1), (2, 2))


def grant(mib):
    return pltpu.CompilerParams(vmem_limit_bytes=mib * 1024 * 1024)


def factors(lev, vel, dif):
    inv = [jnp.left_shift(1, lev[0, d]).astype(F32) for d in range(4)]
    total = sum(vel[d] * inv[d] + 2.0 * dif[d] * inv[d] * inv[d] for d in range(4))
    delta = cfl_limit / jnp.full((1, 128), total, F32)
    adv = [delta * (vel[d] * inv[d]) for d in range(4)]
    dfs = [delta * (dif[d] * inv[d] * inv[d]) for d in range(4)]
    center = 1.0 - sum(adv[d] + 2.0 * dfs[d] for d in range(4))
    return center, [adv[d] + dfs[d] for d in range(4)], dfs


def lane_id(shape):
    return lax.broadcasted_iota(jnp.int32, shape, len(shape) - 1)


def step_row(ref, p, i, fac):
    center, lo, hi = fac
    before, after = lax.rem(p + 15, 16), lax.rem(p + 1, 16)
    u = ref[p, i]
    out = center * u + lo[0] * ref[before, i] + hi[0] * ref[after, i]
    out = out + lo[1] * ref[p, (i + 15) % 16] + hi[1] * ref[p, (i + 1) % 16]
    out = out + lo[2] * pltpu.roll(u, 1, 0) + hi[2] * pltpu.roll(u, 15, 0)
    return out + lo[3] * pltpu.roll(u, 1, 1) + hi[3] * pltpu.roll(u, 127, 1)


def take_slot(packed_ref, slot, out_ref, at):
    for b in range(2):
        for h in range(2):
            out_ref[at, 8 * b : 8 * b + 8, 128 * h : 128 * h + 128] = packed_ref[b, pl.ds(8 * h + slot, 8, stride=16), :]


def put_slot(packed_ref, slot, value):
    for b in range(2):
        for h in range(2):
            packed_ref[b, pl.ds(8 * h + slot, 8, stride=16), :] = value[8 * b : 8 * b + 8, 128 * h : 128 * h + 128]


def ends_kernel(x_ref, lo_ref, hi_ref, mid_ref, packed_ref):
    lane = lane_id((128, 128))
    for b in range(2):
        acc = jnp.zeros((128, 128), F32)
        for c in range(16):
            block = x_ref[8 * b + c // 2, 8 * (c % 2) : 8 * (c % 2) + 8].reshape(128, 128)
            acc = jnp.where(lax.shift_right_logical(lane, 3) == c, pltpu.roll(block, (4 + 8 * c) % 128, 1), acc)
        packed_ref[b] = acc.T
    for slot, (out_ref, at) in enumerate(
        ((mid_ref, 0), (mid_ref, 1), (hi_ref, 0), (hi_ref, 1), (lo_ref, 0), (lo_ref, 1), (lo_ref, 2), (mid_ref, 2))
    ):
        take_slot(packed_ref, slot, out_ref, at)


def first_kernel(lev, vel, dif, x_ref, u_ref):
    fac = factors(lev, vel, dif)

    def plane(p, _):
        for i in range(16):
            u_ref[p, i] = step_row(x_ref, p, i, fac)
        return 0

    lax.fori_loop(0, 16, plane, 0)


def layer_step(u, below, above, center, lo, hi):
    def wide(v):
        return jnp.concatenate([v, v], axis=1)

    lane = lane_id((16, 256)) & 15
    out = wide(center) * u + wide(lo[0]) * pltpu.roll(u, 1, 0) + wide(hi[0]) * pltpu.roll(u, 15, 0)
    out = out + wide(lo[1]) * pltpu.roll(u, 16, 1) + wide(hi[1]) * pltpu.roll(u, 240, 1)
    down = jnp.where(lane == 0, pltpu.roll(u, 241, 1), pltpu.roll(u, 1, 1))
    up = jnp.where(lane == 15, pltpu.roll(u, 15, 1), pltpu.roll(u, 255, 1))
    out = out + wide(lo[2]) * down + wide(hi[2]) * up
    return out + wide(lo[3]) * below + wide(hi[3]) * above


def layers_kernel(lev, vel, dif, wgt, pos, lo_ref, hi_ref, mid_ref, left_ref, right_ref, edge_ref, shared_ref, packed_ref):
    fac = factors(lev, vel, dif)
    weight = wgt[0].astype(F32)

    def step(seq):
        return [layer_step(seq[k], seq[k - 1], seq[k + 1], *fac) for k in range(1, len(seq) - 1)]

    low = step(step([left_ref[0], left_ref[1], lo_ref[0], lo_ref[1], lo_ref[2], mid_ref[2]]))
    high = step(step([mid_ref[0], mid_ref[1], hi_ref[0], hi_ref[1], right_ref[0], right_ref[1], right_ref[2]]))
    packed_ref[...] = jnp.zeros_like(packed_ref)
    for slot, value in enumerate((high[0], high[1], low[0], low[1], high[2])):
        put_slot(packed_ref, slot, weight * value)
    edge_ref[...] = packed_ref[...].reshape(256, 128)
    shared = jnp.where((pos[1] & 1) == 1, weight * high[2], weight * low[0])
    shared_ref[0:16] = shared[:, :128]
    shared_ref[16:32] = shared[:, 128:]


def partners(y):
    return y, y ^ 1, 3 - y, y ^ 2


def second_kernel(chunk, lev, vel, dif, wgt, pos, u_ref, edge_ref, shared_ref, *outs):
    fac = factors(lev, vel, dif)
    weight = wgt[0].astype(F32)
    for target, out_ref in zip(partners(pos[0]), outs):

        def body(r, _, target=target, out_ref=out_ref):
            p = 4 * target + CHUNKS[chunk][0] + r
            base = pl.multiple_of(272 * r, 16)
            for i in range(16):
                out_ref[pl.ds(base + 16 * i, 16), :] = weight * step_row(u_ref, p, i, fac)
            out_ref[pl.ds(base + 256, 16), :] = edge_ref[pl.ds(pl.multiple_of(16 * p, 16), 16), :]
            return 0

        lax.fori_loop(0, CHUNKS[chunk][1], body, 0)
        if chunk == 0:
            out_ref[272 * CHUNKS[0][1] :] = shared_ref[...]


def surplus_rows(planes, a_ref, b_ref, mat_ref, o_ref, at, packed_ref):
    for n in range(planes):
        rows = slice(272 * n + 256, 272 * n + 272)
        packed_ref[16 * n : 16 * n + 16] = a_ref[rows] + b_ref[rows]
    turned = packed_ref[...].T
    lane = lane_id((1, 128))
    edge = (lane < 2) | (lane > 125)
    ramp = lane.astype(F32) * (1.0 / 128.0)
    for n in range(planes):
        for h in range(2):
            rows = slice(272 * n + 128 * h, 272 * n + 128 * h + 128)
            ends = pltpu.roll(turned, 126 - 8 * (2 * n + h), 1)
            full = jnp.where(edge, ends, a_ref[rows] + b_ref[rows]) - ramp * ends[:, 2:3]
            o_ref[at + 256 * n + 128 * h : at + 256 * n + 128 * h + 128] = jnp.dot(
                full, mat_ref[...], precision=lax.Precision.HIGHEST, preferred_element_type=F32
            )


def surplus_pair_kernel(a_ref, b_ref, c_ref, d_ref, mat_ref, o_ref, packed_ref):
    packed_ref[...] = jnp.zeros_like(packed_ref)
    surplus_rows(1, a_ref, b_ref, mat_ref, o_ref, 0, packed_ref)
    surplus_rows(1, c_ref, d_ref, mat_ref, o_ref, 256, packed_ref)


def surplus_fix_kernel(pos, table, a_ref, b_ref, mat_ref, shared_ref, *rest):
    got, (o_ref, packed_ref) = rest[:-2], rest[-2:]
    packed_ref[...] = jnp.zeros_like(packed_ref)
    surplus_rows(2, a_ref, b_ref, mat_ref, o_ref, 0, packed_ref)
    at = 32 * pos[0] + pos[1]
    fix = table[len(got), at] * shared_ref[...]
    for k, ref in enumerate(got):
        fix = fix + table[k, at] * ref[...]
    o_ref[512:] = fix


def last_kernel(pos, *refs):
    pieces, (out_ref, packed_ref, turned_ref, block_ref, sems) = (refs[:4], refs[4:8]), refs[8:]
    fix = sum(ref[512:] for ref in pieces[1])
    for b in range(2):
        for h in range(2):
            packed_ref[b, pl.ds(8 * h, 8, stride=16), :] = fix[16 * h + 8 * b : 16 * h + 8 * b + 8]
        turned_ref[b] = packed_ref[b].T
    first = lane_id((1, 128)) == 0
    copies = []
    for half in range(2):
        for t, target in enumerate(partners(pos[0])):
            turned = turned_ref[lax.shift_right_logical(target, 1)]
            at = 8 * half + 2 * t
            for r in range(2):
                for h in range(2):
                    k = (2 * (4 * target + 2 * half + r) + h) & 15
                    fixed = pltpu.roll(turned, (128 - 8 * k) & 127, 1)
                    rows = slice(256 * r + 128 * h, 256 * r + 128 * h + 128)
                    part = pieces[half][t][rows, :] + jnp.where(first, fixed, 0.0)
                    block_ref[at + r, 8 * h : 8 * h + 8] = part.reshape(8, 16, 128)
            copy = pltpu.make_async_copy(
                block_ref.at[pl.ds(at, 2)], out_ref.at[pl.ds(4 * target + 2 * half, 2)], sems.at[4 * half + t]
            )
            copy.start()
            copies.append(copy)
    for copy in copies:
        copy.wait()


def surplus_matrix():
    m = np.eye(128, dtype=np.float32)
    for j in range(1, 128):
        s = j & -j
        m[j - s, j] -= 0.5
        if j + s < 128:
            m[j + s, j] -= 0.5
    return m


def after(value, *others):
    return lax.optimization_barrier((value,) + others)[0]


def tree_edges(n, replicas):
    edges = []
    for b in range(1, n):
        s = b & -b
        if s == 1:
            edges.append((b - 1, b, -0.5))
        elif (b + s) % n == b - s:
            edges.append((b - s, b, -1.0))
        else:
            edges += [(b - s, b, -0.5), ((b + s) % n, b, -0.5)]
    degree = [sum(e[0] == b for e in edges) for b in range(n)]
    colours = max(degree + [sum(e[1] == b for e in edges) for b in range(n)])
    colours = -(-colours // replicas) * replicas
    out, into, used = {}, {}, {}

    def swap_path(v, side, c, d):
        path, here, colour = [], (side, v), c
        while True:
            key = (out if here[0] == 0 else into).get((here[1], colour))
            if key is None:
                break
            path.append((key, colour))
            here = (1 - here[0], key[1] if here[0] == 0 else key[0])
            colour = d if colour == c else c
        for key, col in path:
            del out[(key[0], col)], into[(key[1], col)]
        for key, col in path:
            new = d if col == c else c
            out[(key[0], new)] = into[(key[1], new)] = key
            used[key] = new

    for src, dst, _ in sorted(edges, key=lambda e: (-degree[e[0]], e)):
        free_src = [c for c in range(colours) if (src, c) not in out]
        free_dst = [c for c in range(colours) if (dst, c) not in into]
        both = [c for c in free_src if c in free_dst]
        colour = both[0] if both else free_src[0]
        if not both:
            swap_path(dst, 1, colour, free_dst[0])
        out[(src, colour)] = into[(dst, colour)] = (src, dst)
        used[(src, dst)] = colour
    count = colours // replicas
    rounds = [[] for _ in range(count)]
    table = np.zeros((count + 1, replicas * n), np.float32)
    for src, dst, factor in edges:
        k, y = divmod(used[(src, dst)], replicas)
        rounds[k].append((y * n + src, y * n + dst))
        table[k, y * n + dst] = factor
    table[count, 1:n:2] = -0.5
    return rounds, table


def local(initial, levels, weights, velocity, diffusivity):
    others = [[(i, partners(i)[k]) for i in range(4)] for k in (1, 2, 3)]
    pair = [(0, 1), (1, 0)]
    n = lax.axis_size(BRICK)
    up = [(i, (i + 1) % n) for i in range(n)]
    down = [(i, (i - 1) % n) for i in range(n)]
    x = initial[0]
    pos = jnp.stack([lax.axis_index("y"), lax.axis_index(BRICK)]).astype(jnp.int32)
    scalars = (levels, velocity, diffusivity, weights, pos)

    def struct(*shape):
        return jax.ShapeDtypeStruct(shape, F32)

    lo, hi, mid = pl.pallas_call(
        ends_kernel,
        out_shape=(struct(3, 16, 256), struct(2, 16, 256), struct(3, 16, 256)),
        in_specs=[VM],
        out_specs=(VM,) * 3,
        scratch_shapes=[pltpu.VMEM((2, 128, 128), F32)],
        compiler_params=grant(4),
    )(x)
    left = lax.ppermute(hi, BRICK, up)
    right = lax.ppermute(lo, BRICK, down)
    cost = pl.CostEstimate(flops=10000000, bytes_accessed=4 << 20, transcendentals=0)
    u = pl.pallas_call(
        first_kernel,
        out_shape=struct(*x.shape),
        in_specs=[SM] * 3 + [VM],
        out_specs=VM,
        compiler_params=grant(6),
        cost_estimate=cost,
    )(levels, velocity, diffusivity, x)
    left, right = after((left, right), u)
    edges, shared = pl.pallas_call(
        layers_kernel,
        out_shape=(struct(256, 128), struct(32, 128)),
        scratch_shapes=[pltpu.VMEM((2, 128, 128), F32)],
        in_specs=[SM] * 5 + [VM] * 5,
        out_specs=(VM,) * 2,
        compiler_params=grant(2),
    )(*scalars, lo, hi, mid, left, right)

    def second(c, value):
        return pl.pallas_call(
            functools.partial(second_kernel, c),
            out_shape=(struct(272 * CHUNKS[c][1] + (0 if c else 32), 128),) * 4,
            in_specs=[SM] * 5 + [VM] * 3,
            out_specs=(VM,) * 4,
            compiler_params=grant(5),
            cost_estimate=cost,
        )(*scalars, value, edges, shared)

    def to_others(values):
        return [lax.ppermute(value, "y", perm) for value, perm in zip(values, others)]

    def surplus(kernel, out, *args, scalar=0):
        return pl.pallas_call(
            kernel,
            out_shape=out,
            in_specs=[SM] * scalar + [VM] * (len(args) - scalar),
            out_specs=jax.tree.map(lambda _: VM, out),
            scratch_shapes=[pltpu.VMEM((128, 128), F32)],
            compiler_params=grant(3),
        )(*args)

    matrix = jnp.asarray(surplus_matrix())
    rounds, table = tree_edges(n, 4)
    value, gate, summed, partner = u, (), [], []
    for c in range(3):
        parts = second(c, value)
        value = after(u, parts[0])
        got = to_others(after(parts[1:], *gate))
        summed.append(parts[0] + got[0] + got[1] + got[2])
        gate = (summed[0],) if c else ()
        partner.append(lax.ppermute(summed[c], "zh", pair))
    shared = summed[0][-32:] + partner[0][-32:]
    got = [lax.ppermute(shared, ("y",) + BRICK, r) for r in rounds]
    own0 = surplus(
        surplus_pair_kernel,
        struct(512, 128),
        summed[0],
        partner[0],
        summed[1],
        after(partner[1], summed[2]),
        matrix,
    )
    pieces0 = [own0] + to_others([own0] * 3)
    own1 = surplus(
        surplus_fix_kernel,
        struct(544, 128),
        pos,
        jnp.asarray(table),
        summed[2],
        after(partner[2], *pieces0),
        matrix,
        shared,
        *got,
        scalar=2,
    )
    pieces1 = [own1] + to_others([own1] * 3)
    return pl.pallas_call(
        last_kernel,
        out_shape=struct(16, 16, 16, 128),
        in_specs=[SM] + [VM] * 8,
        out_specs=pl.BlockSpec(memory_space=pl.ANY),
        scratch_shapes=[
            pltpu.VMEM((2, 128, 128), F32),
            pltpu.VMEM((2, 128, 128), F32),
            pltpu.VMEM((16, 16, 16, 128), F32),
            pltpu.SemaphoreType.DMA((8,)),
        ],
        compiler_params=grant(6),
    )(pos, *pieces0, *pieces1)


def solution(mesh):
    wide = Mesh(mesh.devices.reshape(2, 4, 4, 4, 2), ("zh", "y", "x", "zl", "core"))
    comp = ("zh", "y")
    return jax.shard_map(
        local,
        mesh=wide,
        in_specs=(P(comp, None, None, None, BRICK), P(comp, None), P(comp), P(), P()),
        out_specs=P(None, None, None, BRICK),
        check_vma=False,
    )
```

```python
import functools
import jax
import jax.numpy as jnp
import numpy as np
from jax import lax
from jax.experimental import pallas as pl
from jax.experimental.pallas import tpu as pltpu
from jax.sharding import Mesh, PartitionSpec as P

cfl_limit = 0.9
BRICK = ("x", "zl", "core")
VM = pl.BlockSpec(memory_space=pltpu.VMEM)
SM = pl.BlockSpec(memory_space=pltpu.SMEM)
F32 = jnp.float32
CHUNKS = ((0, 1), (1, 1), (2, 2))


def grant(mib):
    return pltpu.CompilerParams(vmem_limit_bytes=mib * 1024 * 1024)


def factors(lev, vel, dif):
    inv = [jnp.left_shift(1, lev[0, d]).astype(F32) for d in range(4)]
    total = sum(vel[d] * inv[d] + 2.0 * dif[d] * inv[d] * inv[d] for d in range(4))
    delta = cfl_limit / jnp.full((1, 128), total, F32)
    adv = [delta * (vel[d] * inv[d]) for d in range(4)]
    dfs = [delta * (dif[d] * inv[d] * inv[d]) for d in range(4)]
    center = 1.0 - sum(adv[d] + 2.0 * dfs[d] for d in range(4))
    return center, [adv[d] + dfs[d] for d in range(4)], dfs


def lane_id(shape):
    return lax.broadcasted_iota(jnp.int32, shape, len(shape) - 1)


def step_row(ref, p, i, fac):
    center, lo, hi = fac
    before, after = lax.rem(p + 15, 16), lax.rem(p + 1, 16)
    u = ref[p, i]
    out = center * u + lo[0] * ref[before, i] + hi[0] * ref[after, i]
    out = out + lo[1] * ref[p, (i + 15) % 16] + hi[1] * ref[p, (i + 1) % 16]
    out = out + lo[2] * pltpu.roll(u, 1, 0) + hi[2] * pltpu.roll(u, 15, 0)
    return out + lo[3] * pltpu.roll(u, 1, 1) + hi[3] * pltpu.roll(u, 127, 1)


def take_slot(packed_ref, slot, out_ref, at):
    for b in range(2):
        for h in range(2):
            out_ref[at, 8 * b : 8 * b + 8, 128 * h : 128 * h + 128] = packed_ref[b, pl.ds(8 * h + slot, 8, stride=16), :]


def put_slot(packed_ref, slot, value):
    for b in range(2):
        for h in range(2):
            packed_ref[b, pl.ds(8 * h + slot, 8, stride=16), :] = value[8 * b : 8 * b + 8, 128 * h : 128 * h + 128]


def ends_kernel(x_ref, lo_ref, hi_ref, mid_ref, packed_ref):
    lane = lane_id((128, 128))
    for b in range(2):
        acc = jnp.zeros((128, 128), F32)
        for c in range(16):
            block = x_ref[8 * b + c // 2, 8 * (c % 2) : 8 * (c % 2) + 8].reshape(128, 128)
            acc = jnp.where(lax.shift_right_logical(lane, 3) == c, pltpu.roll(block, (4 + 8 * c) % 128, 1), acc)
        packed_ref[b] = acc.T
    for slot, (out_ref, at) in enumerate(
        ((mid_ref, 0), (mid_ref, 1), (hi_ref, 0), (hi_ref, 1), (lo_ref, 0), (lo_ref, 1), (lo_ref, 2), (mid_ref, 2))
    ):
        take_slot(packed_ref, slot, out_ref, at)


def first_kernel(lev, vel, dif, x_ref, u_ref):
    fac = factors(lev, vel, dif)

    def planes(k, _):
        for j in range(4):
            for i in range(16):
                u_ref[4 * k + j, i] = step_row(x_ref, 4 * k + j, i, fac)
        return 0

    lax.fori_loop(0, 4, planes, 0)


def layer_step(u, below, above, center, lo, hi):
    def wide(v):
        return jnp.concatenate([v, v], axis=1)

    lane = lane_id((16, 256)) & 15
    out = wide(center) * u + wide(lo[0]) * pltpu.roll(u, 1, 0) + wide(hi[0]) * pltpu.roll(u, 15, 0)
    out = out + wide(lo[1]) * pltpu.roll(u, 16, 1) + wide(hi[1]) * pltpu.roll(u, 240, 1)
    down = jnp.where(lane == 0, pltpu.roll(u, 241, 1), pltpu.roll(u, 1, 1))
    up = jnp.where(lane == 15, pltpu.roll(u, 15, 1), pltpu.roll(u, 255, 1))
    out = out + wide(lo[2]) * down + wide(hi[2]) * up
    return out + wide(lo[3]) * below + wide(hi[3]) * above


def layers_kernel(lev, vel, dif, wgt, pos, lo_ref, hi_ref, mid_ref, left_ref, right_ref, edge_ref, shared_ref, packed_ref):
    fac = factors(lev, vel, dif)
    weight = wgt[0].astype(F32)

    def step(seq):
        return [layer_step(seq[k], seq[k - 1], seq[k + 1], *fac) for k in range(1, len(seq) - 1)]

    low = step(step([left_ref[0], left_ref[1], lo_ref[0], lo_ref[1], lo_ref[2], mid_ref[2]]))
    high = step(step([mid_ref[0], mid_ref[1], hi_ref[0], hi_ref[1], right_ref[0], right_ref[1], right_ref[2]]))
    packed_ref[...] = jnp.zeros_like(packed_ref)
    for slot, value in enumerate((high[0], high[1], low[0], low[1], high[2])):
        put_slot(packed_ref, slot, weight * value)
    edge_ref[...] = packed_ref[...].reshape(256, 128)
    shared = jnp.where((pos[1] & 1) == 1, weight * high[2], weight * low[0])
    shared_ref[0:16] = shared[:, :128]
    shared_ref[16:32] = shared[:, 128:]


def partners(y):
    return y, y ^ 1, 3 - y, y ^ 2


def second_kernel(chunk, lev, vel, dif, wgt, pos, u_ref, edge_ref, shared_ref, *outs):
    weight = wgt[0].astype(F32)
    center, lo, hi = factors(lev, vel, dif)
    fac = (weight * center, [weight * v for v in lo], [weight * v for v in hi])
    for target, out_ref in zip(partners(pos[0]), outs):

        def body(r, _, target=target, out_ref=out_ref):
            p = 4 * target + CHUNKS[chunk][0] + r
            base = pl.multiple_of(272 * r, 16)
            for i in range(16):
                out_ref[pl.ds(base + 16 * i, 16), :] = step_row(u_ref, p, i, fac)
            out_ref[pl.ds(base + 256, 16), :] = edge_ref[pl.ds(pl.multiple_of(16 * p, 16), 16), :]
            return 0

        for r in range(CHUNKS[chunk][1]):
            body(r, 0)
        if chunk == 0:
            out_ref[272 * CHUNKS[0][1] :] = shared_ref[...]


def surplus_rows(planes, a_ref, b_ref, mat_ref, o_ref, at, packed_ref):
    for n in range(planes):
        rows = slice(272 * n + 256, 272 * n + 272)
        packed_ref[16 * n : 16 * n + 16] = a_ref[rows] + b_ref[rows]
    turned = packed_ref[...].T
    lane = lane_id((1, 128))
    edge = (lane < 2) | (lane > 125)
    ramp = lane.astype(F32) * (1.0 / 128.0)
    for n in range(planes):
        for h in range(2):
            rows = slice(272 * n + 128 * h, 272 * n + 128 * h + 128)
            ends = pltpu.roll(turned, 126 - 8 * (2 * n + h), 1)
            full = jnp.where(edge, ends, a_ref[rows] + b_ref[rows]) - ramp * ends[:, 2:3]
            o_ref[at + 256 * n + 128 * h : at + 256 * n + 128 * h + 128] = jnp.dot(
                full, mat_ref[...], precision=lax.Precision.HIGHEST, preferred_element_type=F32
            )


def surplus_pair_kernel(a_ref, b_ref, c_ref, d_ref, mat_ref, o_ref, packed_ref):
    packed_ref[...] = jnp.zeros_like(packed_ref)
    surplus_rows(1, a_ref, b_ref, mat_ref, o_ref, 0, packed_ref)
    surplus_rows(1, c_ref, d_ref, mat_ref, o_ref, 256, packed_ref)


def surplus_fix_kernel(pos, table, a_ref, b_ref, mat_ref, shared_ref, *rest):
    got, (o_ref, packed_ref) = rest[:-2], rest[-2:]
    packed_ref[...] = jnp.zeros_like(packed_ref)
    surplus_rows(2, a_ref, b_ref, mat_ref, o_ref, 0, packed_ref)
    at = 32 * pos[0] + pos[1]
    fix = table[len(got), at] * shared_ref[...]
    for k, ref in enumerate(got):
        fix = fix + table[k, at] * ref[...]
    o_ref[512:] = fix


def last_kernel(pos, *refs):
    pieces, (out_ref, packed_ref, turned_ref, block_ref, sems) = (refs[:4], refs[4:8]), refs[8:]
    fix = sum(ref[512:] for ref in pieces[1])
    for b in range(2):
        for h in range(2):
            packed_ref[b, pl.ds(8 * h, 8, stride=16), :] = fix[16 * h + 8 * b : 16 * h + 8 * b + 8]
        turned_ref[b] = packed_ref[b].T
    first = lane_id((1, 128)) == 0
    copies = []
    for half in range(2):
        for t, target in enumerate(partners(pos[0])):
            turned = turned_ref[lax.shift_right_logical(target, 1)]
            at = 8 * half + 2 * t
            for r in range(2):
                for h in range(2):
                    k = (2 * (4 * target + 2 * half + r) + h) & 15
                    fixed = pltpu.roll(turned, (128 - 8 * k) & 127, 1)
                    rows = slice(256 * r + 128 * h, 256 * r + 128 * h + 128)
                    part = pieces[half][t][rows, :] + jnp.where(first, fixed, 0.0)
                    block_ref[at + r, 8 * h : 8 * h + 8] = part.reshape(8, 16, 128)
            copy = pltpu.make_async_copy(
                block_ref.at[pl.ds(at, 2)], out_ref.at[pl.ds(4 * target + 2 * half, 2)], sems.at[4 * half + t]
            )
            copy.start()
            copies.append(copy)
    for copy in copies:
        copy.wait()


def surplus_matrix():
    m = np.eye(128, dtype=np.float32)
    for j in range(1, 128):
        s = j & -j
        m[j - s, j] -= 0.5
        if j + s < 128:
            m[j + s, j] -= 0.5
    return m


def after(value, *others):
    return lax.optimization_barrier((value,) + others)[0]


def tree_edges(n, replicas):
    edges = []
    for b in range(1, n):
        s = b & -b
        if s == 1:
            edges.append((b - 1, b, -0.5))
        elif (b + s) % n == b - s:
            edges.append((b - s, b, -1.0))
        else:
            edges += [(b - s, b, -0.5), ((b + s) % n, b, -0.5)]
    degree = [sum(e[0] == b for e in edges) for b in range(n)]
    colours = max(degree + [sum(e[1] == b for e in edges) for b in range(n)])
    colours = -(-colours // replicas) * replicas
    out, into, used = {}, {}, {}

    def swap_path(v, side, c, d):
        path, here, colour = [], (side, v), c
        while True:
            key = (out if here[0] == 0 else into).get((here[1], colour))
            if key is None:
                break
            path.append((key, colour))
            here = (1 - here[0], key[1] if here[0] == 0 else key[0])
            colour = d if colour == c else c
        for key, col in path:
            del out[(key[0], col)], into[(key[1], col)]
        for key, col in path:
            new = d if col == c else c
            out[(key[0], new)] = into[(key[1], new)] = key
            used[key] = new

    for src, dst, _ in sorted(edges, key=lambda e: (-degree[e[0]], e)):
        free_src = [c for c in range(colours) if (src, c) not in out]
        free_dst = [c for c in range(colours) if (dst, c) not in into]
        both = [c for c in free_src if c in free_dst]
        colour = both[0] if both else free_src[0]
        if not both:
            swap_path(dst, 1, colour, free_dst[0])
        out[(src, colour)] = into[(dst, colour)] = (src, dst)
        used[(src, dst)] = colour
    count = colours // replicas
    rounds = [[] for _ in range(count)]
    table = np.zeros((count + 1, replicas * n), np.float32)
    for src, dst, factor in edges:
        k, y = divmod(used[(src, dst)], replicas)
        rounds[k].append((y * n + src, y * n + dst))
        table[k, y * n + dst] = factor
    table[count, 1:n:2] = -0.5
    return rounds, table


def local(initial, levels, weights, velocity, diffusivity):
    others = [[(i, partners(i)[k]) for i in range(4)] for k in (1, 2, 3)]
    pair = [(0, 1), (1, 0)]
    n = lax.axis_size(BRICK)
    up = [(i, (i + 1) % n) for i in range(n)]
    down = [(i, (i - 1) % n) for i in range(n)]
    x = initial[0]
    pos = jnp.stack([lax.axis_index("y"), lax.axis_index(BRICK)]).astype(jnp.int32)
    scalars = (levels, velocity, diffusivity, weights, pos)

    def struct(*shape):
        return jax.ShapeDtypeStruct(shape, F32)

    lo, hi, mid = pl.pallas_call(
        ends_kernel,
        out_shape=(struct(3, 16, 256), struct(2, 16, 256), struct(3, 16, 256)),
        in_specs=[VM],
        out_specs=(VM,) * 3,
        scratch_shapes=[pltpu.VMEM((2, 128, 128), F32)],
        compiler_params=grant(4),
    )(x)
    left = lax.ppermute(hi, BRICK, up)
    right = lax.ppermute(lo, BRICK, down)
    cost = pl.CostEstimate(flops=10000000, bytes_accessed=4 << 20, transcendentals=0)
    u = pl.pallas_call(
        first_kernel,
        out_shape=struct(*x.shape),
        in_specs=[SM] * 3 + [VM],
        out_specs=VM,
        compiler_params=grant(6),
        cost_estimate=cost,
    )(levels, velocity, diffusivity, x)
    left, right = after((left, right), u)
    edges, shared = pl.pallas_call(
        layers_kernel,
        out_shape=(struct(256, 128), struct(32, 128)),
        scratch_shapes=[pltpu.VMEM((2, 128, 128), F32)],
        in_specs=[SM] * 5 + [VM] * 5,
        out_specs=(VM,) * 2,
        compiler_params=grant(2),
    )(*scalars, lo, hi, mid, left, right)

    def second(c, value):
        return pl.pallas_call(
            functools.partial(second_kernel, c),
            out_shape=(struct(272 * CHUNKS[c][1] + (0 if c else 32), 128),) * 4,
            in_specs=[SM] * 5 + [VM] * 3,
            out_specs=(VM,) * 4,
            compiler_params=grant(5),
            cost_estimate=cost,
        )(*scalars, value, edges, shared)

    def to_others(values):
        return [lax.ppermute(value, "y", perm) for value, perm in zip(values, others)]

    def surplus(kernel, out, *args, scalar=0):
        return pl.pallas_call(
            kernel,
            out_shape=out,
            in_specs=[SM] * scalar + [VM] * (len(args) - scalar),
            out_specs=jax.tree.map(lambda _: VM, out),
            scratch_shapes=[pltpu.VMEM((128, 128), F32)],
            compiler_params=grant(3),
        )(*args)

    matrix = jnp.asarray(surplus_matrix())
    rounds, table = tree_edges(n, 4)
    value, gate, summed, partner = u, (), [], []
    for c in range(3):
        parts = second(c, value)
        value = after(u, parts[0])
        got = to_others(after(parts[1:], *gate))
        if c == 1:
            got = after(got, partner[0])
        summed.append(parts[0] + got[0] + got[1] + got[2])
        gate = (summed[0],) if c else ()
        partner.append(lax.ppermute(summed[c], "zh", pair))
    shared = summed[0][-32:] + partner[0][-32:]
    got = [lax.ppermute(shared, ("y",) + BRICK, r) for r in rounds]
    own0 = surplus(
        surplus_pair_kernel,
        struct(512, 128),
        summed[0],
        partner[0],
        summed[1],
        after(partner[1], summed[2]),
        matrix,
    )
    pieces0 = [own0] + to_others([own0] * 3)
    own1 = surplus(
        surplus_fix_kernel,
        struct(544, 128),
        pos,
        jnp.asarray(table),
        summed[2],
        after(partner[2], *pieces0),
        matrix,
        shared,
        *got,
        scalar=2,
    )
    pieces1 = [own1] + to_others([own1] * 3)
    return pl.pallas_call(
        last_kernel,
        out_shape=struct(16, 16, 16, 128),
        in_specs=[SM] + [VM] * 8,
        out_specs=pl.BlockSpec(memory_space=pl.ANY),
        scratch_shapes=[
            pltpu.VMEM((2, 128, 128), F32),
            pltpu.VMEM((2, 128, 128), F32),
            pltpu.VMEM((16, 16, 16, 128), F32),
            pltpu.SemaphoreType.DMA((8,)),
        ],
        compiler_params=grant(6),
    )(pos, *pieces0, *pieces1)


def solution(mesh):
    wide = Mesh(mesh.devices.reshape(2, 4, 4, 4, 2), ("zh", "y", "x", "zl", "core"))
    comp = ("zh", "y")
    return jax.shard_map(
        local,
        mesh=wide,
        in_specs=(P(comp, None, None, None, BRICK), P(comp, None), P(comp), P(), P()),
        out_specs=P(None, None, None, BRICK),
        check_vma=False,
    )
```

```python
import functools
import jax
import jax.numpy as jnp
import numpy as np
from jax import lax
from jax.experimental import pallas as pl
from jax.experimental.pallas import tpu as pltpu
from jax.sharding import Mesh, PartitionSpec as P

cfl_limit = 0.9
BRICK = ("x", "zl", "core")
VM = pl.BlockSpec(memory_space=pltpu.VMEM)
SM = pl.BlockSpec(memory_space=pltpu.SMEM)
F32 = jnp.float32
CHUNKS = ((0, 1), (1, 1), (2, 2))


def grant(mib):
    return pltpu.CompilerParams(vmem_limit_bytes=mib * 1024 * 1024)


def factors(lev, vel, dif):
    inv = [jnp.left_shift(1, lev[0, d]).astype(F32) for d in range(4)]
    total = sum(vel[d] * inv[d] + 2.0 * dif[d] * inv[d] * inv[d] for d in range(4))
    delta = cfl_limit / jnp.full((1, 128), total, F32)
    adv = [delta * (vel[d] * inv[d]) for d in range(4)]
    dfs = [delta * (dif[d] * inv[d] * inv[d]) for d in range(4)]
    center = 1.0 - sum(adv[d] + 2.0 * dfs[d] for d in range(4))
    return center, [adv[d] + dfs[d] for d in range(4)], dfs


def lane_id(shape):
    return lax.broadcasted_iota(jnp.int32, shape, len(shape) - 1)


def step_row(ref, p, i, fac):
    center, lo, hi = fac
    before, after = lax.rem(p + 15, 16), lax.rem(p + 1, 16)
    u = ref[p, i]
    out = center * u + lo[0] * ref[before, i] + hi[0] * ref[after, i]
    out = out + lo[1] * ref[p, (i + 15) % 16] + hi[1] * ref[p, (i + 1) % 16]
    out = out + lo[2] * pltpu.roll(u, 1, 0) + hi[2] * pltpu.roll(u, 15, 0)
    return out + lo[3] * pltpu.roll(u, 1, 1) + hi[3] * pltpu.roll(u, 127, 1)


def take_slot(packed_ref, slot, out_ref, at):
    for b in range(2):
        for h in range(2):
            out_ref[at, 8 * b : 8 * b + 8, 128 * h : 128 * h + 128] = packed_ref[b, pl.ds(8 * h + slot, 8, stride=16), :]


def put_slot(packed_ref, slot, value):
    for b in range(2):
        for h in range(2):
            packed_ref[b, pl.ds(8 * h + slot, 8, stride=16), :] = value[8 * b : 8 * b + 8, 128 * h : 128 * h + 128]


def ends_kernel(x_ref, lo_ref, hi_ref, mid_ref, packed_ref):
    lane = lane_id((128, 128))
    for b in range(2):
        acc = jnp.zeros((128, 128), F32)
        for c in range(16):
            block = x_ref[8 * b + c // 2, 8 * (c % 2) : 8 * (c % 2) + 8].reshape(128, 128)
            acc = jnp.where(lax.shift_right_logical(lane, 3) == c, pltpu.roll(block, (4 + 8 * c) % 128, 1), acc)
        packed_ref[b] = acc.T
    for slot, (out_ref, at) in enumerate(
        ((mid_ref, 0), (mid_ref, 1), (hi_ref, 0), (hi_ref, 1), (lo_ref, 0), (lo_ref, 1), (lo_ref, 2), (mid_ref, 2))
    ):
        take_slot(packed_ref, slot, out_ref, at)


def first_kernel(lev, vel, dif, x_ref, u_ref):
    fac = factors(lev, vel, dif)

    def planes(k, _):
        for j in range(4):
            for i in range(16):
                u_ref[4 * k + j, i] = step_row(x_ref, 4 * k + j, i, fac)
        return 0

    lax.fori_loop(0, 4, planes, 0)


def layer_step(u, below, above, center, lo, hi):
    def wide(v):
        return jnp.concatenate([v, v], axis=1)

    lane = lane_id((16, 256)) & 15
    out = wide(center) * u + wide(lo[0]) * pltpu.roll(u, 1, 0) + wide(hi[0]) * pltpu.roll(u, 15, 0)
    out = out + wide(lo[1]) * pltpu.roll(u, 16, 1) + wide(hi[1]) * pltpu.roll(u, 240, 1)
    down = jnp.where(lane == 0, pltpu.roll(u, 241, 1), pltpu.roll(u, 1, 1))
    up = jnp.where(lane == 15, pltpu.roll(u, 15, 1), pltpu.roll(u, 255, 1))
    out = out + wide(lo[2]) * down + wide(hi[2]) * up
    return out + wide(lo[3]) * below + wide(hi[3]) * above


def layers_kernel(lev, vel, dif, wgt, pos, lo_ref, hi_ref, mid_ref, left_ref, right_ref, edge_ref, shared_ref, packed_ref):
    fac = factors(lev, vel, dif)
    weight = wgt[0].astype(F32)

    def step(seq):
        return [layer_step(seq[k], seq[k - 1], seq[k + 1], *fac) for k in range(1, len(seq) - 1)]

    low = step(step([left_ref[0], left_ref[1], lo_ref[0], lo_ref[1], lo_ref[2], mid_ref[2]]))
    high = step(step([mid_ref[0], mid_ref[1], hi_ref[0], hi_ref[1], right_ref[0], right_ref[1], right_ref[2]]))
    packed_ref[...] = jnp.zeros_like(packed_ref)
    for slot, value in enumerate((high[0], high[1], low[0], low[1], high[2])):
        put_slot(packed_ref, slot, weight * value)
    edge_ref[...] = packed_ref[...].reshape(256, 128)
    shared = jnp.where((pos[1] & 1) == 1, weight * high[2], weight * low[0])
    shared_ref[0:16] = shared[:, :128]
    shared_ref[16:32] = shared[:, 128:]


def partners(y):
    return y, y ^ 1, 3 - y, y ^ 2


def second_kernel(chunk, lev, vel, dif, wgt, pos, u_ref, edge_ref, shared_ref, *outs):
    weight = wgt[0].astype(F32)
    center, lo, hi = factors(lev, vel, dif)
    fac = (weight * center, [weight * v for v in lo], [weight * v for v in hi])
    for target, out_ref in zip(partners(pos[0]), outs):

        def body(r, _, target=target, out_ref=out_ref):
            p = 4 * target + CHUNKS[chunk][0] + r
            base = pl.multiple_of(272 * r, 16)
            for i in range(16):
                out_ref[pl.ds(base + 16 * i, 16), :] = step_row(u_ref, p, i, fac)
            out_ref[pl.ds(base + 256, 16), :] = edge_ref[pl.ds(pl.multiple_of(16 * p, 16), 16), :]
            return 0

        for r in range(CHUNKS[chunk][1]):
            body(r, 0)
        if chunk == 0:
            out_ref[272 * CHUNKS[0][1] :] = shared_ref[...]


def surplus_rows(planes, a_ref, b_ref, mat_ref, o_ref, at, packed_ref):
    for n in range(planes):
        rows = slice(272 * n + 256, 272 * n + 272)
        packed_ref[16 * n : 16 * n + 16] = a_ref[rows] + b_ref[rows]
    turned = packed_ref[...].T
    lane = lane_id((1, 128))
    edge = (lane < 2) | (lane > 125)
    ramp = lane.astype(F32) * (1.0 / 128.0)
    for n in range(planes):
        for h in range(2):
            rows = slice(272 * n + 128 * h, 272 * n + 128 * h + 128)
            ends = pltpu.roll(turned, 126 - 8 * (2 * n + h), 1)
            full = jnp.where(edge, ends, a_ref[rows] + b_ref[rows]) - ramp * ends[:, 2:3]
            o_ref[at + 256 * n + 128 * h : at + 256 * n + 128 * h + 128] = jnp.dot(
                full, mat_ref[...], precision=lax.Precision.HIGHEST, preferred_element_type=F32
            )


def surplus_pair_kernel(a_ref, b_ref, c_ref, d_ref, mat_ref, o_ref, packed_ref):
    packed_ref[...] = jnp.zeros_like(packed_ref)
    surplus_rows(1, a_ref, b_ref, mat_ref, o_ref, 0, packed_ref)
    surplus_rows(1, c_ref, d_ref, mat_ref, o_ref, 256, packed_ref)


def surplus_fix_kernel(a_ref, b_ref, mat_ref, fix_ref, o_ref, packed_ref):
    packed_ref[...] = jnp.zeros_like(packed_ref)
    surplus_rows(2, a_ref, b_ref, mat_ref, o_ref, 0, packed_ref)
    o_ref[512:] = fix_ref[...]


def last_kernel(pos, *refs):
    pieces, (out_ref, packed_ref, turned_ref, block_ref, sems) = (refs[:4], refs[4:8]), refs[8:]
    fix = sum(ref[512:] for ref in pieces[1])
    for b in range(2):
        for h in range(2):
            packed_ref[b, pl.ds(8 * h, 8, stride=16), :] = fix[16 * h + 8 * b : 16 * h + 8 * b + 8]
        turned_ref[b] = packed_ref[b].T
    first = lane_id((1, 128)) == 0
    copies = []
    for half in range(2):
        for t, target in enumerate(partners(pos[0])):
            turned = turned_ref[lax.shift_right_logical(target, 1)]
            at = 8 * half + 2 * t
            for r in range(2):
                for h in range(2):
                    k = (2 * (4 * target + 2 * half + r) + h) & 15
                    fixed = pltpu.roll(turned, (128 - 8 * k) & 127, 1)
                    rows = slice(256 * r + 128 * h, 256 * r + 128 * h + 128)
                    part = pieces[half][t][rows, :] + jnp.where(first, fixed, 0.0)
                    block_ref[at + r, 8 * h : 8 * h + 8] = part.reshape(8, 16, 128)
            copy = pltpu.make_async_copy(
                block_ref.at[pl.ds(at, 2)], out_ref.at[pl.ds(4 * target + 2 * half, 2)], sems.at[4 * half + t]
            )
            copy.start()
            copies.append(copy)
    for copy in copies:
        copy.wait()


def surplus_matrix():
    m = np.eye(128, dtype=np.float32)
    for j in range(1, 128):
        s = j & -j
        m[j - s, j] -= 0.5
        if j + s < 128:
            m[j + s, j] -= 0.5
    return m


def after(value, *others):
    return lax.optimization_barrier((value,) + others)[0]


def tree_edges(n, replicas):
    edges = []
    for b in range(1, n):
        s = b & -b
        if s == 1:
            edges.append((b - 1, b, -0.5))
        elif (b + s) % n == b - s:
            edges.append((b - s, b, -1.0))
        else:
            edges += [(b - s, b, -0.5), ((b + s) % n, b, -0.5)]
    degree = [sum(e[0] == b for e in edges) for b in range(n)]
    colours = max(degree + [sum(e[1] == b for e in edges) for b in range(n)])
    colours = -(-colours // replicas) * replicas
    out, into, used = {}, {}, {}

    def swap_path(v, side, c, d):
        path, here, colour = [], (side, v), c
        while True:
            key = (out if here[0] == 0 else into).get((here[1], colour))
            if key is None:
                break
            path.append((key, colour))
            here = (1 - here[0], key[1] if here[0] == 0 else key[0])
            colour = d if colour == c else c
        for key, col in path:
            del out[(key[0], col)], into[(key[1], col)]
        for key, col in path:
            new = d if col == c else c
            out[(key[0], new)] = into[(key[1], new)] = key
            used[key] = new

    for src, dst, _ in sorted(edges, key=lambda e: (-degree[e[0]], e)):
        free_src = [c for c in range(colours) if (src, c) not in out]
        free_dst = [c for c in range(colours) if (dst, c) not in into]
        both = [c for c in free_src if c in free_dst]
        colour = both[0] if both else free_src[0]
        if not both:
            swap_path(dst, 1, colour, free_dst[0])
        out[(src, colour)] = into[(dst, colour)] = (src, dst)
        used[(src, dst)] = colour
    count = colours // replicas
    rounds = [[] for _ in range(count)]
    table = np.zeros((count + 1, replicas * n), np.float32)
    for src, dst, factor in edges:
        k, y = divmod(used[(src, dst)], replicas)
        rounds[k].append((y * n + src, y * n + dst))
        table[k, y * n + dst] = factor
    table[count, 1:n:2] = -0.5
    return rounds, table


def local(initial, levels, weights, velocity, diffusivity):
    others = [[(i, partners(i)[k]) for i in range(4)] for k in (1, 2, 3)]
    pair = [(0, 1), (1, 0)]
    n = lax.axis_size(BRICK)
    up = [(i, (i + 1) % n) for i in range(n)]
    down = [(i, (i - 1) % n) for i in range(n)]
    x = initial[0]
    pos = jnp.stack([lax.axis_index("y"), lax.axis_index(BRICK)]).astype(jnp.int32)
    scalars = (levels, velocity, diffusivity, weights, pos)

    def struct(*shape):
        return jax.ShapeDtypeStruct(shape, F32)

    lo, hi, mid = pl.pallas_call(
        ends_kernel,
        out_shape=(struct(3, 16, 256), struct(2, 16, 256), struct(3, 16, 256)),
        in_specs=[VM],
        out_specs=(VM,) * 3,
        scratch_shapes=[pltpu.VMEM((2, 128, 128), F32)],
        compiler_params=grant(4),
    )(x)
    left = lax.ppermute(hi, BRICK, up)
    right = lax.ppermute(lo, BRICK, down)
    cost = pl.CostEstimate(flops=10000000, bytes_accessed=4 << 20, transcendentals=0)
    u = pl.pallas_call(
        first_kernel,
        out_shape=struct(*x.shape),
        in_specs=[SM] * 3 + [VM],
        out_specs=VM,
        compiler_params=grant(6),
        cost_estimate=cost,
    )(levels, velocity, diffusivity, x)
    left, right = after((left, right), u)
    edges, shared = pl.pallas_call(
        layers_kernel,
        out_shape=(struct(256, 128), struct(32, 128)),
        scratch_shapes=[pltpu.VMEM((2, 128, 128), F32)],
        in_specs=[SM] * 5 + [VM] * 5,
        out_specs=(VM,) * 2,
        compiler_params=grant(2),
    )(*scalars, lo, hi, mid, left, right)

    def second(c, value):
        return pl.pallas_call(
            functools.partial(second_kernel, c),
            out_shape=(struct(272 * CHUNKS[c][1] + (0 if c else 32), 128),) * 4,
            in_specs=[SM] * 5 + [VM] * 3,
            out_specs=(VM,) * 4,
            compiler_params=grant(5),
            cost_estimate=cost,
        )(*scalars, value, edges, shared)

    def to_others(values):
        return [lax.ppermute(value, "y", perm) for value, perm in zip(values, others)]

    def surplus(kernel, out, *args, scalar=0):
        return pl.pallas_call(
            kernel,
            out_shape=out,
            in_specs=[SM] * scalar + [VM] * (len(args) - scalar),
            out_specs=jax.tree.map(lambda _: VM, out),
            scratch_shapes=[pltpu.VMEM((128, 128), F32)],
            compiler_params=grant(3),
        )(*args)

    matrix = jnp.asarray(surplus_matrix())
    rounds, table = tree_edges(n, 4)
    value, gate, summed, partner = u, (), [], []
    for c in range(3):
        parts = second(c, value)
        value = after(u, parts[0])
        got = to_others(after(parts[1:], *gate))
        if c == 1:
            got = after(got, partner[0])
        summed.append(parts[0] + got[0] + got[1] + got[2])
        gate = (summed[0],) if c else ()
        partner.append(lax.ppermute(summed[c], "zh", pair))
    shared = summed[0][-32:] + partner[0][-32:]
    got = [lax.ppermute(shared, ("y",) + BRICK, r) for r in rounds]
    own0 = surplus(
        surplus_pair_kernel,
        struct(512, 128),
        summed[0],
        partner[0],
        summed[1],
        after(partner[1], summed[2]),
        matrix,
    )
    pieces0 = [own0] + to_others([own0] * 3)
    factor = jnp.asarray(table)[:, 32 * pos[0] + pos[1]]
    fix = factor[len(got)] * shared + sum(factor[k] * value for k, value in enumerate(got))
    own1 = surplus(
        surplus_fix_kernel, struct(544, 128), summed[2], after(partner[2], *pieces0), matrix, fix
    )
    pieces1 = [own1] + to_others([own1] * 3)
    return pl.pallas_call(
        last_kernel,
        out_shape=struct(16, 16, 16, 128),
        in_specs=[SM] + [VM] * 8,
        out_specs=pl.BlockSpec(memory_space=pl.ANY),
        scratch_shapes=[
            pltpu.VMEM((2, 128, 128), F32),
            pltpu.VMEM((2, 128, 128), F32),
            pltpu.VMEM((16, 16, 16, 128), F32),
            pltpu.SemaphoreType.DMA((8,)),
        ],
        compiler_params=grant(6),
    )(pos, *pieces0, *pieces1)


def solution(mesh):
    wide = Mesh(mesh.devices.reshape(2, 4, 4, 4, 2), ("zh", "y", "x", "zl", "core"))
    comp = ("zh", "y")
    return jax.shard_map(
        local,
        mesh=wide,
        in_specs=(P(comp, None, None, None, BRICK), P(comp, None), P(comp), P(), P()),
        out_specs=P(None, None, None, BRICK),
        check_vma=False,
    )
```
